32 devices in a mesh: scene: 8 (over y, x, core), kd: 4 (over z).
Axes of the slice: x: 2, y: 2, z: 4, core: 2. Of those that a mesh axis runs over, the one named last changes fastest.
Arguments:
- features: bfloat16 [8, 16, 512, 128], P('scene', 'kd'), may hold values from -6 to 6
- send_faces: int32 [8, 4, 2, 1], P('scene', 'kd'), may hold values from 0 to 23, as said below
- face_source: int32 [8, 16, 6], P('scene', 'kd'), may hold values from 0 to 26, as said below
- cotangent: bfloat16 [8, 16, 64, 256], P('scene', 'kd'), may hold values from -8 to 8
- conv_one: bfloat16 [7, 128, 128], replicated, may hold values from -0.1875 to 0.1875
- down_weight: bfloat16 [1024, 256], replicated, may hold values from -0.1875 to 0.1875
- conv_two: bfloat16 [7, 256, 256], replicated, may hold values from -0.125 to 0.125
Outputs:
- encoded: bfloat16 [8, 16, 64, 256], P('scene', 'kd')
- grad_conv_one: float32 [7, 128, 128], replicated
- grad_down: float32 [1024, 256], replicated
- grad_conv_two: float32 [7, 256, 256], replicated
The draws below stay inside these ranges and needn't reach their ends.
Inputs may be any that keep to these rules, and one draw needn't show every extreme that they name: `send_faces`: entry [i, t] names face 6 b + s of the sender's own brick b; across bit i every device sends exactly one face, of side 2 (i mod 3) + 1 where its bit i is 0 and of side 2 (i mod 3) where it is 1; no face is named twice on a device. `face_source`: for brick b and direction s: a value under 6 * 4 is a local face, of the side opposite s; 24 + i + t is slot t received across bit i; 26 is no neighbour. The relation is symmetric: where direction s of brick b takes a face of brick b2, direction opposite s of b2 takes the face of b at side s, across devices through the same bit and slot.
All inputs are finite; a program needn't handle non-finite values.
Results may differ from the reference program's by a relative error of at most 0.0065.
Values may be sent and summed in bfloat16 or wider, within the bound.
A program may use at most 64 MiB of HBM per device.

```python
import jax
import jax.numpy as jnp
from jax import lax

C1 = 128
C2 = 256
BRICKS = 4
SLOTS = 1
NBITS = 2
SCENES = 8
NB = 16
N_KD = 4


def brick_lists(key):
    empty_slot = 6 * BRICKS + NBITS * SLOTS

    def one_device(device_key, device):
        shuffled = jax.random.permutation(jax.random.fold_in(device_key, 1), BRICKS).astype(jnp.int32)
        source = jnp.full((BRICKS * 6,), empty_slot, jnp.int32)
        outgoing = []
        for bit_index in range(NBITS):
            axis_id = bit_index % 3
            upper_side = jnp.bitwise_and(jnp.right_shift(device, bit_index), 1)
            face_ids = shuffled[bit_index * SLOTS:(bit_index + 1) * SLOTS] * 6 + 2 * axis_id + 1 - upper_side
            outgoing.append(face_ids)
            source = source.at[face_ids].set(6 * BRICKS + bit_index * SLOTS + jnp.arange(SLOTS, dtype=jnp.int32))
        for axis_id in range(3):
            chain_order = jax.random.permutation(jax.random.fold_in(device_key, 10 + axis_id), BRICKS).astype(jnp.int32)
            keep_mask = jax.random.randint(jax.random.fold_in(device_key, 20 + axis_id), (BRICKS - 1,), 0, 4) > 0
            plus_ids = chain_order[:-1] * 6 + 2 * axis_id + 1
            minus_ids = chain_order[1:] * 6 + 2 * axis_id
            plus_old = source[plus_ids]
            minus_old = source[minus_ids]
            linked = keep_mask & (plus_old == empty_slot) & (minus_old == empty_slot)
            source = source.at[plus_ids].set(jnp.where(linked, minus_ids, plus_old))
            source = source.at[minus_ids].set(jnp.where(linked, plus_ids, minus_old))
        return (jnp.stack(outgoing), source.reshape(BRICKS, 6))

    def one_scene(scene):
        scene_key = jax.random.fold_in(jax.random.fold_in(key, 977), scene)
        return jax.vmap(lambda device: one_device(jax.random.fold_in(scene_key, device), device))(jnp.arange(N_KD, dtype=jnp.int32))
    outgoing, source = jax.vmap(one_scene)(jnp.arange(SCENES, dtype=jnp.int32))
    return (outgoing, source.reshape(SCENES, N_KD * BRICKS, 6))


def draw_send_faces(key, part):
    return brick_lists(key)[0]


def draw_face_source(key, part):
    return brick_lists(key)[1]


def spiked(entries, stream_key, source, target, parts, factor):
    def block_of(position):
        return (jnp.arange(entries.shape[position]) // (entries.shape[position] // parts)).reshape((-1,) + (1,) * (entries.ndim - 1 - position))

    one_side = jax.random.permutation(stream_key, parts)[block_of(target)]
    other_side = (block_of(target) + parts // 2) % parts
    return jnp.where((block_of(source) == one_side) | (block_of(source) == other_side), factor * entries, entries)


def level_of(rng, dims, pieces, smallest, high):
    gain, own = 1.0, jax.random.fold_in(rng, 6)
    for dim, shards_of in pieces:
        heights = jnp.exp(jax.random.uniform(jax.random.fold_in(own, dim), (shards_of,), jnp.float32, smallest / len(pieces), high / len(pieces)))
        gain = gain * jnp.repeat(heights, dims[dim] // shards_of).reshape([-1 if axis == dim else 1 for axis in range(len(dims))])
    return gain


def normal_values(key, shape, deviation, reach, split=(), kind=jnp.bfloat16):
    entries = deviation * jax.random.normal(key, shape, jnp.float32)
    if split:
        entries = entries * level_of(key, shape, split, -0.22, 0.18)
    return jnp.clip(entries, -reach, reach).astype(kind)


def noise_with(own_key, extent, width, most, pieces, heavy, kind=jnp.bfloat16):
    result = width * jax.random.normal(own_key, extent, jnp.float32)
    if pieces:
        result = result * level_of(own_key, extent, pieces, -0.22, 0.18)
    return jnp.clip(spiked(result, jax.random.fold_in(own_key, 3), *heavy), -most, most).astype(kind)


def setup_inputs(seed: int = 0) -> dict:
    keys = jax.random.split(jax.random.key(seed), 8)
    return {
        "features": normal_values(keys[0], (SCENES, NB, 512, C1), 1.0, 6.0, ((0, 8), (1, 4))),
        "send_faces": draw_send_faces(jax.random.fold_in(keys[7], 71), 0),
        "face_source": draw_face_source(jax.random.fold_in(keys[7], 71), 0),
        "cotangent": noise_with(keys[3], (SCENES, NB, 64, C2), 1.0, 8.0, ((0, 8), (1, 4)), (0, 3, 8, 2.0)),
        "conv_one": normal_values(keys[4], (7, C1, C1), (7 * C1) ** -0.5, 0.1875),
        "down_weight": normal_values(keys[5], (8 * C1, C2), (8 * C1) ** -0.5, 0.1875),
        "conv_two": normal_values(keys[6], (7, C2, C2), (7 * C2) ** -0.5, 0.125),
    }


OPPOSITE = (0, 2, 1, 4, 3, 6, 5)


def face_slabs(blocks):
    return jnp.stack([blocks[:, 0], blocks[:, -1], blocks[:, :, 0], blocks[:, :, -1], blocks[:, :, :, 0], blocks[:, :, :, -1]], axis=1)


def shift_taps(blocks, border):
    return [
        blocks,
        jnp.concatenate([border[:, 0][:, None], blocks[:, :-1]], 1),
        jnp.concatenate([blocks[:, 1:], border[:, 1][:, None]], 1),
        jnp.concatenate([border[:, 2][:, :, None], blocks[:, :, :-1]], 2),
        jnp.concatenate([blocks[:, :, 1:], border[:, 3][:, :, None]], 2),
        jnp.concatenate([border[:, 4][:, :, :, None], blocks[:, :, :, :-1]], 3),
        jnp.concatenate([blocks[:, :, :, 1:], border[:, 5][:, :, :, None]], 3),
    ]


def conv_apply(taps, weight):
    chans = taps[0].shape[-1]
    total = jnp.dot(taps[0].reshape(-1, chans), weight[0], preferred_element_type=jnp.float32)
    for tap_index in range(1, 7):
        total = total + jnp.dot(taps[tap_index].reshape(-1, chans), weight[tap_index], preferred_element_type=jnp.float32)
    return total


def conv_back(taps, weight):
    chans = taps[0].shape[-1]
    total = lax.dot_general(taps[0].reshape(-1, chans), weight[0], (((1,), (1,)), ((), ())), preferred_element_type=jnp.float32)
    for tap_index in range(1, 7):
        total = total + lax.dot_general(taps[OPPOSITE[tap_index]].reshape(-1, chans), weight[tap_index], (((1,), (1,)), ((), ())), preferred_element_type=jnp.float32)
    return total


def weight_grads(taps, delta):
    chans = taps[0].shape[-1]
    return jnp.stack([lax.dot_general(single.reshape(-1, chans), delta, (((0,), (0,)), ((), ())), preferred_element_type=jnp.float32) for single in taps])


def down_rows(hidden, brick_count, chans):
    return hidden.reshape(brick_count, 4, 2, 4, 2, 4, 2, chans).transpose(0, 1, 3, 5, 2, 4, 6, 7).reshape(brick_count * 64, 8 * chans)


def up_rows(patch_grad, brick_count, chans):
    return patch_grad.reshape(brick_count, 4, 4, 4, 2, 2, 2, chans).transpose(0, 1, 4, 2, 5, 3, 6, 7).reshape(brick_count * 512, chans)


def silu_slope(value):
    sigma = jax.nn.sigmoid(value)
    return sigma * (1.0 + value * (1.0 - sigma))


def scene_rims(blocks, scene_send, scene_source):
    devices = scene_send.shape[0]
    per_device = blocks.shape[0] // devices
    side_cells = blocks.shape[1]
    chans = blocks.shape[-1]
    faces = face_slabs(blocks).reshape(devices, per_device * 6, side_cells, side_cells, chans)
    outgoing = jax.vmap(lambda face_table, chosen: face_table[chosen])(faces, scene_send)
    device_ids = jnp.arange(devices, dtype=jnp.int32)
    incoming = jnp.stack([outgoing[jnp.bitwise_xor(device_ids, 1 << bit_index), bit_index] for bit_index in range(scene_send.shape[1])], axis=1)
    incoming = incoming.reshape(devices, -1, side_cells, side_cells, chans)
    empty = jnp.zeros((devices, 1, side_cells, side_cells, chans), blocks.dtype)
    lookup = jnp.concatenate([faces, incoming, empty], axis=1)
    border = jax.vmap(lambda device_table, chosen: device_table[chosen])(lookup, scene_source.reshape(devices, per_device, 6))
    return border.reshape(devices * per_device, 6, side_cells, side_cells, chans)


def reference(features, send_faces, face_source, cotangent, conv_one, down_weight, conv_two):
    def scene_pass(carry, inputs):
        scene_feat, scene_send, scene_source, scene_cot = inputs
        brick_count = scene_feat.shape[0]
        chan_one = scene_feat.shape[-1]
        chan_two = scene_cot.shape[-1]
        grid_one = scene_feat.reshape(brick_count, 8, 8, 8, chan_one)
        taps_one = shift_taps(grid_one, scene_rims(grid_one, scene_send, scene_source))
        pre_one = conv_apply(taps_one, conv_one)
        hidden_one = (scene_feat.reshape(-1, chan_one).astype(jnp.float32) + jax.nn.silu(pre_one)).astype(jnp.bfloat16)
        patches = down_rows(hidden_one, brick_count, chan_one)
        coarse = jnp.dot(patches, down_weight, preferred_element_type=jnp.float32).astype(jnp.bfloat16)
        grid_two = coarse.reshape(brick_count, 4, 4, 4, chan_two)
        taps_two = shift_taps(grid_two, scene_rims(grid_two, scene_send, scene_source))
        pre_two = conv_apply(taps_two, conv_two)
        encoded = (coarse.astype(jnp.float32) + jax.nn.silu(pre_two)).astype(jnp.bfloat16)
        upstream = scene_cot.reshape(-1, chan_two).astype(jnp.float32)
        delta_two = (upstream * silu_slope(pre_two)).astype(jnp.bfloat16)
        grid_delta = delta_two.reshape(brick_count, 4, 4, 4, chan_two)
        taps_delta = shift_taps(grid_delta, scene_rims(grid_delta, scene_send, scene_source))
        grad_coarse = (upstream + conv_back(taps_delta, conv_two)).astype(jnp.bfloat16)
        patch_grad = lax.dot_general(grad_coarse, down_weight, (((1,), (1,)), ((), ())), preferred_element_type=jnp.float32)
        delta_one = (up_rows(patch_grad, brick_count, chan_one) * silu_slope(pre_one)).astype(jnp.bfloat16)
        grad_one, grad_down, grad_two = carry
        grad_one = grad_one + weight_grads(taps_one, delta_one)
        grad_down = grad_down + lax.dot_general(patches, grad_coarse, (((0,), (0,)), ((), ())), preferred_element_type=jnp.float32)
        grad_two = grad_two + weight_grads(taps_two, delta_two)
        return (grad_one, grad_down, grad_two), encoded.reshape(brick_count, 64, chan_two)

    start = (jnp.zeros((7, C1, C1), jnp.float32), jnp.zeros((8 * C1, C2), jnp.float32), jnp.zeros((7, C2, C2), jnp.float32))
    grads, encoded = lax.scan(scene_pass, start, (features, send_faces, face_source, cotangent))
    return encoded, grads[0], grads[1], grads[2]
```

```python
import functools

import jax
import jax.numpy as jnp
from jax import lax
from jax.experimental import pallas as pl
from jax.experimental.pallas import tpu as pltpu
from jax.sharding import PartitionSpec as P

MESH = pl.DeviceIdType.MESH
F32 = jnp.float32
BF16 = jnp.bfloat16
STRIDE = (16, 4, 1)
CLASS = (4, 2, 1)
OPPOSITE = (0, 2, 1, 4, 3, 6, 5)


def dot(a, b):
    return jnp.dot(a, b, preferred_element_type=F32)


def dot_tn(a, b):
    return lax.dot_general(a, b, (((0,), (0,)), ((), ())), preferred_element_type=F32)


def dot_nt(a, b):
    return lax.dot_general(a, b, (((1,), (1,)), ((), ())), preferred_element_type=F32)


def one_hot(mask):
    return jnp.where(mask, 1.0, 0.0).astype(BF16)


def sigmoid(v):
    return 0.5 * jnp.tanh(0.5 * v) + 0.5


def coordinate(row, axis):
    return (row // STRIDE[axis]) % 4


def face_rows(row, axis):
    first, second = [a for a in range(3) if a != axis]
    return coordinate(row, first) * 4 + coordinate(row, second)


def lanes(ref, classes):
    return jnp.concatenate([ref[:, c * 128 : (c + 1) * 128] for c in classes], axis=1)


class Reduction:
    def __init__(self, total, staged, landed, out, sems, bits, n_scene, n_kd):
        self.total, self.staged, self.landed, self.out = total, staged, landed, out
        self.send, self.recv = sems
        self.bits, self.n_kd = bits, n_kd
        self.piece = total.shape[0] // (n_scene * n_kd)
        self.scene = lax.axis_index("scene")
        self.kd = lax.axis_index("kd")
        self.sem = 0
        self.base = 0
        self.count = n_scene * n_kd
        self.offset = 0
        self.levels = []
        self.copies = []

    def rows(self, start, count):
        return pl.ds(pl.multiple_of(start * self.piece, 16), count * self.piece)

    def copy(self, src, dst, device):
        made = pltpu.make_async_remote_copy(
            src_ref=src,
            dst_ref=dst,
            send_sem=self.send.at[self.sem],
            recv_sem=self.recv.at[self.sem],
            device_id=device,
            device_id_type=MESH,
        )
        self.sem += 1
        made.start()
        return made

    def steps(self):
        for bit in self.bits:
            mask = 2**bit
            mine = (self.scene // mask) % 2
            half = self.count // 2
            other = {"scene": self.scene + mask - 2 * mask * mine}
            away = self.offset + (1 - mine) * half
            keep = self.offset + mine * half
            slot = pl.ds(self.base * self.piece, half * self.piece)
            self.staged[slot, :] = self.total[self.rows(away, half), :].astype(BF16)
            made = self.copy(self.staged.at[slot], self.landed.at[slot], other)
            yield
            made.wait()
            kept = self.rows(keep, half)
            self.total[kept, :] = self.total[kept, :] + self.landed[slot, :].astype(F32)
            self.base += half
            self.count = half
            self.offset = keep
            self.levels.append((other, keep, half))
        made = []
        for j in range(1, self.n_kd):
            peer = self.peer(j)
            slot = pl.ds(self.base * self.piece, self.piece)
            self.staged[slot, :] = self.total[self.rows(self.offset + peer, 1), :].astype(BF16)
            made.append((self.copy(self.staged.at[slot], self.landed.at[slot], {"kd": peer}), slot))
            self.base += 1
        yield
        own = self.rows(self.offset + self.kd, 1)
        value = self.total[own, :]
        for one, slot in made:
            one.wait()
            value = value + self.landed[slot, :].astype(F32)
        self.out[own, :] = value.astype(BF16)
        made = [
            self.copy(self.out.at[own], self.out.at[own], {"kd": self.peer(j)})
            for j in range(1, self.n_kd)
        ]
        yield
        for one in made:
            one.wait()
        for other, keep, half in reversed(self.levels):
            kept = self.rows(keep, half)
            one = self.copy(self.out.at[kept], self.out.at[kept], other)
            yield
            one.wait()

    def peer(self, j):
        result = self.kd
        bit = 1
        while bit < self.n_kd:
            if j & bit:
                result = result + bit - 2 * bit * ((self.kd // bit) % 2)
            bit *= 2
        return result


def kernel(
    n_scene,
    n_kd,
    n_bits,
    x_ref,
    send_ref,
    source_ref,
    cot_ref,
    w1_ref,
    dw_ref,
    w2_ref,
    enc_ref,
    out0_ref,
    out1_ref,
    xp_ref,
    t1_ref,
    slope_ref,
    patch_ref,
    shift_ref,
    place_ref,
    pick_ref,
    t2_ref,
    fs1,
    fr1,
    fs2,
    fr2,
    fs3,
    fr3,
    face_send,
    face_recv,
    tot0,
    stage0,
    land0,
    send0,
    recv0,
    tot1,
    stage1,
    land1,
    send1,
    recv1,
):
    bricks = source_ref.shape[0]
    rows = bricks * 64
    local = bricks * 6
    scene_bits = n_scene.bit_length() - 1
    kd = lax.axis_index("kd")
    scene = lax.axis_index("scene")
    order = list(range(scene_bits))
    sum0 = Reduction(tot0, stage0, land0, out0_ref, (send0, recv0), order, n_scene, n_kd)
    sum1 = Reduction(
        tot1, stage1, land1, out1_ref, (send1, recv1), order[:1] + order[:0:-1], n_scene, n_kd
    )

    barrier = pltpu.get_barrier_semaphore()
    for j in range(1, n_kd):
        pl.semaphore_signal(barrier, inc=1, device_id={"kd": sum0.peer(j)}, device_id_type=MESH)
    for bit in range(scene_bits):
        mask = 2**bit
        other = scene + mask - 2 * mask * ((scene // mask) % 2)
        pl.semaphore_signal(barrier, inc=1, device_id={"scene": other}, device_id_type=MESH)

    to = lax.broadcasted_iota(jnp.int32, (128, 128), 0)
    frm = lax.broadcasted_iota(jnp.int32, (128, 128), 1)
    wanted = (
        (to // 64) * 64
        + (2 * ((to // 4) % 4) + (to // 32) % 2) * 8
        + 2 * (to % 4)
        + (to // 16) % 2
    )
    arrange = one_hot(frm == wanted)
    for block in range(rows // 16):
        moved = dot(arrange, x_ref[block * 128 : (block + 1) * 128, :]).astype(BF16)
        for c in range(8):
            xp_ref[block * 16 : (block + 1) * 16, c * 128 : (c + 1) * 128] = moved[
                c * 16 : (c + 1) * 16
            ]

    face = lax.broadcasted_iota(jnp.int32, (16, rows), 0)
    voxel = lax.broadcasted_iota(jnp.int32, (16, rows), 1)
    for bit in range(n_bits):
        axis = bit % 3
        mine = (kd // 2**bit) % 2
        first, second = [a for a in range(3) if a != axis]
        at = (
            (send_ref[bit, 0] // 6) * 64
            + 3 * STRIDE[axis] * (1 - mine)
            + (face // 4) * STRIDE[first]
            + (face % 4) * STRIDE[second]
        )
        pick_ref[bit * 16 : (bit + 1) * 16, :] = one_hot(voxel == at)

    def exchange(stage, send_buf, recv_buf, pieces):
        copies = []
        for bit in range(n_bits):
            send_buf[bit] = pieces[bit].astype(BF16)
            made = pltpu.make_async_remote_copy(
                src_ref=send_buf.at[bit],
                dst_ref=recv_buf.at[bit],
                send_sem=face_send.at[stage * n_bits + bit],
                recv_sem=face_recv.at[stage * n_bits + bit],
                device_id={"kd": sum0.peer(2**bit)},
                device_id_type=MESH,
            )
            made.start()
            copies.append(made)
        return copies

    far = {}
    for axis in range(3):
        high = [c for c in range(8) if c & CLASS[axis]]
        low = [c for c in range(8) if not c & CLASS[axis]]
        far[2 * axis], far[2 * axis + 1] = high, low
    picked = dot(pick_ref[...], xp_ref[...])
    pieces = []
    for bit in range(n_bits):
        axis = bit % 3
        mine = (kd // 2**bit) % 2
        part = picked[bit * 16 : (bit + 1) * 16]
        pieces.append(
            jnp.where(mine == 0, lanes(part, far[2 * axis]), lanes(part, far[2 * axis + 1]))
        )
    pl.semaphore_wait(barrier, n_kd - 1 + scene_bits)
    copies = exchange(0, fs1, fr1, pieces)

    row = lax.broadcasted_iota(jnp.int32, (64, rows), 0)
    col = lax.broadcasted_iota(jnp.int32, (64, rows), 1)
    row16 = lax.broadcasted_iota(jnp.int32, (64, 16), 0)
    col16 = lax.broadcasted_iota(jnp.int32, (64, 16), 1)
    for s in range(6):
        axis, step = s // 2, STRIDE[s // 2]
        sign = 1 if s % 2 else -1
        edge = 3 if s % 2 else 0
        for b in range(bricks):
            source = source_ref[b, s]
            border = coordinate(row, axis) == edge
            base = jnp.where(source < local, (source // 6) * 64, -4096)
            at = row + jnp.where(border, base - sign * 3 * step, b * 64 + sign * step)
            shift_ref[s, b * 64 : (b + 1) * 64, :] = one_hot(col == at)
            for bit in range(axis, n_bits, 3):
                here = jnp.where(source == local + bit, 0, -4096)
                slot = jnp.where(
                    coordinate(row16, axis) == edge, face_rows(row16, axis) + here, -4096
                )
                place_ref[bit, s % 2, b * 64 : (b + 1) * 64, :] = one_hot(col16 == slot)

    def shifted(s, operand, arrived):
        value = dot(shift_ref[s], operand)
        for bit in range(s // 2, n_bits, 3):
            value = value + dot(place_ref[bit, s % 2], arrived[bit])
        return value.astype(BF16)

    sides = sorted(range(6), key=lambda s: (s // 2 < n_bits, s))

    for c in range(8):
        t1_ref[c, :, 0:128] = xp_ref[:, c * 128 : (c + 1) * 128]
    for s in range(6):
        tap = slice((s + 1) * 128, (s + 2) * 128)
        for c in far[s]:
            near = c ^ CLASS[s // 2]
            t1_ref[c, :, tap] = xp_ref[:, near * 128 : (near + 1) * 128]
    waited = False
    for s in sides:
        if s // 2 < n_bits and not waited:
            for made in copies:
                made.wait()
            waited = True
        tap = slice((s + 1) * 128, (s + 2) * 128)
        moved = shifted(s, lanes(xp_ref, far[s]), fr1)
        for k, c in enumerate(far[s]):
            t1_ref[c ^ CLASS[s // 2], :, tap] = moved[:, k * 128 : (k + 1) * 128]

    for c in range(8):
        cols = slice(c * 128, (c + 1) * 128)
        pre = dot(t1_ref[c], w1_ref[...])
        g = sigmoid(pre)
        slope_ref[:, cols] = g * (1.0 + pre * (1.0 - g))
        patch_ref[:, cols] = (xp_ref[:, cols].astype(F32) + pre * g).astype(BF16)

    coarse = dot(patch_ref[...], dw_ref[...]).astype(BF16)
    picked = dot(pick_ref[...], coarse)
    copies = exchange(1, fs2, fr2, [picked[i * 16 : (i + 1) * 16] for i in range(n_bits)])
    t2_ref[:, 0:256] = coarse
    waited = False
    for s in sides:
        if s // 2 < n_bits and not waited:
            for made in copies:
                made.wait()
            waited = True
        t2_ref[:, (s + 1) * 256 : (s + 2) * 256] = shifted(s, coarse, fr2)
    pre = dot(t2_ref[...], w2_ref[...])
    g = sigmoid(pre)
    enc_ref[...] = (coarse.astype(F32) + pre * g).astype(BF16)
    upstream = cot_ref[...].astype(F32)
    delta = (upstream * (g * (1.0 + pre * (1.0 - g)))).astype(BF16)
    picked = dot(pick_ref[...], delta)
    copies = exchange(2, fs3, fr3, [picked[i * 16 : (i + 1) * 16] for i in range(n_bits)])

    wide = 7 * 256
    grad_two = dot_tn(t2_ref[...], delta)
    tot0[0:wide, :] = grad_two[:, 0:128]
    tot0[wide : 2 * wide, :] = grad_two[:, 128:256]
    if tot0.shape[0] > 2 * wide:
        tot0[2 * wide :, :] = jnp.zeros((tot0.shape[0] - 2 * wide, 128), F32)
    run0 = sum0.steps()
    next(run0)

    back = upstream + dot_nt(delta, w2_ref[0:256, :])
    waited = False
    for s in sides:
        if s // 2 < n_bits and not waited:
            for made in copies:
                made.wait()
            waited = True
        t = OPPOSITE[s + 1]
        back = back + dot_nt(shifted(s, delta, fr3), w2_ref[t * 256 : (t + 1) * 256, :])
    grad_coarse = back.astype(BF16)
    next(run0)

    high = 8 * 128
    grad_down = dot_tn(patch_ref[...], grad_coarse)
    tot1[0:high, :] = grad_down[:, 0:128]
    tot1[high : 2 * high, :] = grad_down[:, 128:256]
    grad_one = jnp.zeros((7 * 128, 128), F32)
    for c in range(8):
        cols = slice(c * 128, (c + 1) * 128)
        patch_grad = dot_nt(grad_coarse, dw_ref[cols, :])
        delta_one = (patch_grad * slope_ref[:, cols]).astype(BF16)
        grad_one = grad_one + dot_tn(t1_ref[c], delta_one)
    end = 2 * high + 7 * 128
    tot1[2 * high : end, :] = grad_one
    if tot1.shape[0] > end:
        tot1[end:, :] = jnp.zeros((tot1.shape[0] - end, 128), F32)
    run1 = sum1.steps()
    next(run1)
    pending = [run0, run1]
    while pending:
        for run in list(pending):
            if next(run, "end") == "end":
                pending.remove(run)


def padded(rows, devices):
    return -(-rows // (16 * devices)) * 16 * devices


def on_device(n_scene, n_kd, features, send_faces, face_source, cotangent, conv_one, down, conv_two):
    bricks = features.shape[1]
    n_bits = send_faces.shape[2]
    rows = bricks * 64
    devices = n_scene * n_kd
    scene_bits = n_scene.bit_length() - 1
    size0 = padded(2 * 7 * 256, devices)
    size1 = padded(2 * 1024 + 7 * 128, devices)
    n_sems = 2 * scene_bits + 2 * (n_kd - 1)
    vmem = pl.BlockSpec(memory_space=pltpu.VMEM)
    smem = pl.BlockSpec(memory_space=pltpu.SMEM)

    def reduction(size):
        return [
            pltpu.VMEM((size, 128), F32),
            pltpu.VMEM((size, 128), BF16),
            pltpu.VMEM((size, 128), BF16),
            pltpu.SemaphoreType.DMA((n_sems,)),
            pltpu.SemaphoreType.DMA((n_sems,)),
        ]

    encoded, sum0, sum1 = pl.pallas_call(
        functools.partial(kernel, n_scene, n_kd, n_bits),
        out_shape=(
            jax.ShapeDtypeStruct((rows, 256), BF16),
            jax.ShapeDtypeStruct((size0, 128), BF16),
            jax.ShapeDtypeStruct((size1, 128), BF16),
        ),
        in_specs=[vmem, smem, smem, vmem, vmem, vmem, vmem],
        out_specs=(vmem, vmem, vmem),
        scratch_shapes=[
            pltpu.VMEM((rows, 1024), BF16),
            pltpu.VMEM((8, rows, 7 * 128), BF16),
            pltpu.VMEM((rows, 1024), F32),
            pltpu.VMEM((rows, 1024), BF16),
            pltpu.VMEM((6, rows, rows), BF16),
            pltpu.VMEM((n_bits, 2, rows, 16), BF16),
            pltpu.VMEM((n_bits * 16, rows), BF16),
            pltpu.VMEM((rows, 7 * 256), BF16),
            pltpu.VMEM((n_bits, 16, 512), BF16),
            pltpu.VMEM((n_bits, 16, 512), BF16),
            pltpu.VMEM((n_bits, 16, 256), BF16),
            pltpu.VMEM((n_bits, 16, 256), BF16),
            pltpu.VMEM((n_bits, 16, 256), BF16),
            pltpu.VMEM((n_bits, 16, 256), BF16),
            pltpu.SemaphoreType.DMA((3 * n_bits,)),
            pltpu.SemaphoreType.DMA((3 * n_bits,)),
        ]
        + reduction(size0)
        + reduction(size1),
        compiler_params=pltpu.CompilerParams(
            collective_id=0, has_side_effects=True, vmem_limit_bytes=48 * 2**20
        ),
    )(
        features.reshape(bricks * 512, 128),
        send_faces[0, 0],
        face_source[0],
        cotangent.reshape(rows, 256),
        conv_one.reshape(7 * 128, 128),
        down,
        conv_two.reshape(7 * 256, 256),
    )
    wide = 7 * 256
    grad_two = jnp.concatenate([sum0[:wide], sum0[wide : 2 * wide]], axis=1).astype(F32)
    grad_down = jnp.concatenate([sum1[:1024], sum1[1024:2048]], axis=1).astype(F32)
    grad_one = sum1[2048 : 2048 + 7 * 128].astype(F32)
    return (
        encoded.reshape(1, bricks, 64, 256),
        grad_one.reshape(7, 128, 128),
        grad_down,
        grad_two.reshape(7, 256, 256),
    )


def solution(mesh):
    placed = (
        P("scene", "kd", None, None),
        P("scene", "kd", None, None),
        P("scene", "kd", None),
        P("scene", "kd", None, None),
        P(),
        P(),
        P(),
    )
    return jax.shard_map(
        functools.partial(on_device, mesh.shape["scene"], mesh.shape["kd"]),
        mesh=mesh,
        in_specs=placed,
        out_specs=(P("scene", "kd", None, None), P(), P(), P()),
        check_vma=False,
    )
```

```python
import functools

import jax
import jax.numpy as jnp
from jax import lax
from jax.experimental import pallas as pl
from jax.experimental.pallas import tpu as pltpu
from jax.sharding import PartitionSpec as P

MESH = pl.DeviceIdType.MESH
F32 = jnp.float32
BF16 = jnp.bfloat16
STRIDE = (16, 4, 1)
CLASS = (4, 2, 1)
OPPOSITE = (0, 2, 1, 4, 3, 6, 5)


def dot(a, b):
    return jnp.dot(a, b, preferred_element_type=F32)


def dot_tn(a, b):
    return lax.dot_general(a, b, (((0,), (0,)), ((), ())), preferred_element_type=F32)


def dot_nt(a, b):
    return lax.dot_general(a, b, (((1,), (1,)), ((), ())), preferred_element_type=F32)


def one_hot(mask):
    return jnp.where(mask, 1.0, 0.0).astype(BF16)


def sigmoid(v):
    return 0.5 * jnp.tanh(0.5 * v) + 0.5


def coordinate(row, axis):
    return (row // STRIDE[axis]) % 4


def face_rows(row, axis):
    first, second = [a for a in range(3) if a != axis]
    return coordinate(row, first) * 4 + coordinate(row, second)


def lanes(ref, classes):
    return jnp.concatenate([ref[:, c * 128 : (c + 1) * 128] for c in classes], axis=1)


class Reduction:
    def __init__(self, total, staged, landed, out, sems, bits, n_scene, n_kd):
        self.total, self.staged, self.landed, self.out = total, staged, landed, out
        self.send, self.recv = sems
        self.bits, self.n_kd = bits, n_kd
        self.piece = total.shape[0] // (n_scene * n_kd)
        self.scene = lax.axis_index("scene")
        self.kd = lax.axis_index("kd")
        self.sem = 0
        self.base = 0
        self.count = n_scene * n_kd
        self.offset = 0
        self.levels = []
        self.copies = []

    def rows(self, start, count):
        return pl.ds(pl.multiple_of(start * self.piece, 16), count * self.piece)

    def copy(self, src, dst, device):
        made = pltpu.make_async_remote_copy(
            src_ref=src,
            dst_ref=dst,
            send_sem=self.send.at[self.sem],
            recv_sem=self.recv.at[self.sem],
            device_id=device,
            device_id_type=MESH,
        )
        self.sem += 1
        made.start()
        return made

    def steps(self):
        for bit in self.bits:
            mask = 2**bit
            mine = (self.scene // mask) % 2
            half = self.count // 2
            other = {"scene": self.scene + mask - 2 * mask * mine}
            away = self.offset + (1 - mine) * half
            keep = self.offset + mine * half
            slot = pl.ds(self.base * self.piece, half * self.piece)
            self.staged[slot, :] = self.total[self.rows(away, half), :].astype(BF16)
            made = self.copy(self.staged.at[slot], self.landed.at[slot], other)
            yield
            made.wait()
            kept = self.rows(keep, half)
            self.total[kept, :] = self.total[kept, :] + self.landed[slot, :].astype(F32)
            self.base += half
            self.count = half
            self.offset = keep
            self.levels.append((other, keep, half))
        made = []
        for j in range(1, self.n_kd):
            peer = self.peer(j)
            slot = pl.ds(self.base * self.piece, self.piece)
            self.staged[slot, :] = self.total[self.rows(self.offset + peer, 1), :].astype(BF16)
            made.append((self.copy(self.staged.at[slot], self.landed.at[slot], {"kd": peer}), slot))
            self.base += 1
        yield
        own = self.rows(self.offset + self.kd, 1)
        value = self.total[own, :]
        for one, slot in made:
            one.wait()
            value = value + self.landed[slot, :].astype(F32)
        self.out[own, :] = value.astype(BF16)
        made = [
            self.copy(self.out.at[own], self.out.at[own], {"kd": self.peer(j)})
            for j in range(1, self.n_kd)
        ]
        yield
        for one in made:
            one.wait()
        for other, keep, half in reversed(self.levels):
            kept = self.rows(keep, half)
            one = self.copy(self.out.at[kept], self.out.at[kept], other)
            yield
            one.wait()

    def peer(self, j):
        result = self.kd
        bit = 1
        while bit < self.n_kd:
            if j & bit:
                result = result + bit - 2 * bit * ((self.kd // bit) % 2)
            bit *= 2
        return result


def kernel(n_scene, n_kd, n_bits, *refs):
    refs = list(refs)

    def take(count):
        taken = refs[:count]
        del refs[:count]
        return taken

    x_hbm, send_ref, source_ref, cot_hbm, w1_hbm, dw_hbm, w2_hbm = take(7)
    enc_ref, *outs = take(5)
    x_ref, cot_ref, w1_ref, dw_ref, w2_ref, in_sem = take(6)
    xp_ref, t1_ref, t1t_ref, slope_ref, patch_ref, patcht_ref, delta1_ref = take(7)
    shift_ref, place_ref, pick_ref, t2_ref, td_ref = take(5)
    fs1, fr1, fs2, fr2, fs3, fr3, face_send, face_recv = take(8)
    bricks = source_ref.shape[1]
    rows = bricks * 64
    local = bricks * 6
    scene_bits = n_scene.bit_length() - 1
    kd = lax.axis_index("kd")
    scene = lax.axis_index("scene")
    up = list(range(scene_bits))
    chains = []
    for k in range(4):
        total, staged, landed, send, recv = take(5)
        order = up if k % 2 == 0 else up[:1] + up[:0:-1]
        chains.append(
            Reduction(total, staged, landed, outs[k], (send, recv), order, n_scene, n_kd)
        )
    loads = []
    for k, (src, dst) in enumerate(
        ((x_hbm, x_ref), (w1_hbm, w1_ref), (dw_hbm, dw_ref), (w2_hbm, w2_ref), (cot_hbm, cot_ref))
    ):
        loads.append(pltpu.make_async_copy(src, dst, in_sem.at[k]))
        loads[-1].start()
    load_x, load_w1, load_dw, load_w2, load_cot = loads

    barrier = pltpu.get_barrier_semaphore()
    for j in range(1, n_kd):
        peer = chains[0].peer(j)
        pl.semaphore_signal(barrier, inc=1, device_id={"kd": peer}, device_id_type=MESH)
    for bit in range(scene_bits):
        mask = 2**bit
        other = scene + mask - 2 * mask * ((scene // mask) % 2)
        pl.semaphore_signal(barrier, inc=1, device_id={"scene": other}, device_id_type=MESH)

    to = lax.broadcasted_iota(jnp.int32, (128, 128), 0)
    frm = lax.broadcasted_iota(jnp.int32, (128, 128), 1)
    wanted = (
        (to // 64) * 64
        + (2 * ((to // 4) % 4) + (to // 32) % 2) * 8
        + 2 * (to % 4)
        + (to // 16) % 2
    )
    arrange = one_hot(frm == wanted)

    face = lax.broadcasted_iota(jnp.int32, (16, rows), 0)
    voxel = lax.broadcasted_iota(jnp.int32, (16, rows), 1)
    for bit in range(n_bits):
        axis = bit % 3
        mine = (kd // 2**bit) % 2
        first, second = [a for a in range(3) if a != axis]
        at = (
            (send_ref[0, bit] // 6) * 64
            + 3 * STRIDE[axis] * (1 - mine)
            + (face // 4) * STRIDE[first]
            + (face % 4) * STRIDE[second]
        )
        pick_ref[bit * 16 : (bit + 1) * 16, :] = one_hot(voxel == at)

    load_x.wait()
    for block in range(rows // 16):
        moved = dot(arrange, x_ref[block * 128 : (block + 1) * 128, :]).astype(BF16)
        for c in range(8):
            xp_ref[block * 16 : (block + 1) * 16, c * 128 : (c + 1) * 128] = moved[
                c * 16 : (c + 1) * 16
            ]

    def exchange(stage, send_buf, recv_buf, pieces):
        copies = []
        for bit in range(n_bits):
            send_buf[bit] = pieces[bit].astype(BF16)
            made = pltpu.make_async_remote_copy(
                src_ref=send_buf.at[bit],
                dst_ref=recv_buf.at[bit],
                send_sem=face_send.at[stage * n_bits + bit],
                recv_sem=face_recv.at[stage * n_bits + bit],
                device_id={"kd": chains[0].peer(2**bit)},
                device_id_type=MESH,
            )
            made.start()
            copies.append(made)
        return copies

    far = {}
    for axis in range(3):
        far[2 * axis] = [c for c in range(8) if c & CLASS[axis]]
        far[2 * axis + 1] = [c for c in range(8) if not c & CLASS[axis]]
    picked = dot(pick_ref[...], xp_ref[...])
    pieces = []
    for bit in range(n_bits):
        axis = bit % 3
        mine = (kd // 2**bit) % 2
        part = picked[bit * 16 : (bit + 1) * 16]
        pieces.append(
            jnp.where(mine == 0, lanes(part, far[2 * axis]), lanes(part, far[2 * axis + 1]))
        )
    pl.semaphore_wait(barrier, n_kd - 1 + scene_bits)
    copies = exchange(0, fs1, fr1, pieces)

    row = lax.broadcasted_iota(jnp.int32, (64, rows), 0)
    col = lax.broadcasted_iota(jnp.int32, (64, rows), 1)
    row16 = lax.broadcasted_iota(jnp.int32, (64, 16), 0)
    col16 = lax.broadcasted_iota(jnp.int32, (64, 16), 1)
    for s in range(6):
        axis, step = s // 2, STRIDE[s // 2]
        sign = 1 if s % 2 else -1
        border = coordinate(row, axis) == (3 if s % 2 else 0)
        border16 = coordinate(row16, axis) == (3 if s % 2 else 0)
        gap = col - row
        gap16 = col16 - face_rows(row16, axis)
        for b in range(bricks):
            source = source_ref[0, b, s]
            base = jnp.where(source < local, (source // 6) * 64, -4096)
            wish = jnp.where(border, base - sign * 3 * step, b * 64 + sign * step)
            shift_ref[s, b * 64 : (b + 1) * 64, :] = one_hot(gap == wish)
            for bit in range(axis, n_bits, 3):
                here = jnp.where(source == local + bit, 0, -4096)
                wish = jnp.where(border16, here, -4096)
                place_ref[bit, s % 2, b * 64 : (b + 1) * 64, :] = one_hot(gap16 == wish)

    for c in range(8):
        t1_ref[c, :, 0:128] = xp_ref[:, c * 128 : (c + 1) * 128]
    for s in range(6):
        tap = slice((s + 1) * 128, (s + 2) * 128)
        moved = dot(shift_ref[s], lanes(xp_ref, far[s])).astype(BF16)
        for k, c in enumerate(far[s]):
            near = c ^ CLASS[s // 2]
            t1_ref[c, :, tap] = xp_ref[:, near * 128 : (near + 1) * 128]
            t1_ref[near, :, tap] = moved[:, k * 128 : (k + 1) * 128]
    for made in copies:
        made.wait()
    for bit in range(n_bits):
        for s in (2 * (bit % 3), 2 * (bit % 3) + 1):
            tap = slice((s + 1) * 128, (s + 2) * 128)
            moved = dot(place_ref[bit, s % 2], fr1[bit]).astype(BF16)
            for k, c in enumerate(far[s]):
                near = c ^ CLASS[s // 2]
                t1_ref[near, :, tap] = t1_ref[near, :, tap] + moved[:, k * 128 : (k + 1) * 128]

    load_w1.wait()
    pre_one = dot(t1_ref[...].reshape(8 * rows, 7 * 128), w1_ref[...])
    for c in range(8):
        cols = slice(c * 128, (c + 1) * 128)
        pre = pre_one[c * rows : (c + 1) * rows]
        g = sigmoid(pre)
        slope_ref[:, cols] = g * (1.0 + pre * (1.0 - g))
        patch_ref[:, cols] = (xp_ref[:, cols].astype(F32) + pre * g).astype(BF16)

    load_dw.wait()
    coarse = dot(patch_ref[...], dw_ref[...]).astype(BF16)
    picked = dot(pick_ref[...], coarse)
    copies = exchange(1, fs2, fr2, [picked[i * 16 : (i + 1) * 16] for i in range(n_bits)])
    t2_ref[:, 0:256] = coarse
    for s in range(6):
        t2_ref[:, (s + 1) * 256 : (s + 2) * 256] = dot(shift_ref[s], coarse).astype(BF16)
    for c in range(8):
        t1t_ref[:, c * rows : (c + 1) * rows] = t1_ref[c].T
        patcht_ref[c * 128 : (c + 1) * 128, :] = patch_ref[:, c * 128 : (c + 1) * 128].T
    for made in copies:
        made.wait()
    for bit in range(n_bits):
        for s in (2 * (bit % 3), 2 * (bit % 3) + 1):
            tap = slice((s + 1) * 256, (s + 2) * 256)
            t2_ref[:, tap] = t2_ref[:, tap] + dot(place_ref[bit, s % 2], fr2[bit]).astype(BF16)
    load_w2.wait()
    load_cot.wait()
    pre = dot(t2_ref[...], w2_ref[...])
    g = sigmoid(pre)
    enc_ref[...] = (coarse.astype(F32) + pre * g).astype(BF16)
    upstream = cot_ref[...].astype(F32)
    delta = (upstream * (g * (1.0 + pre * (1.0 - g)))).astype(BF16)
    picked = dot(pick_ref[...], delta)
    copies = exchange(2, fs3, fr3, [picked[i * 16 : (i + 1) * 16] for i in range(n_bits)])

    grad_two = dot_tn(t2_ref[...], delta)
    flat = jnp.concatenate([grad_two[:, 0:128], grad_two[:, 128:256]], axis=0)
    fill(chains[0].total, flat[0:CUT])
    fill(chains[1].total, flat[CUT:])
    runs = [chains[0].steps(), chains[1].steps()]
    pump(runs)

    td_ref[:, 0:256] = delta
    for s in range(6):
        t = OPPOSITE[s + 1]
        td_ref[:, t * 256 : (t + 1) * 256] = dot(shift_ref[s], delta).astype(BF16)
    for made in copies:
        made.wait()
    for bit in range(n_bits):
        for s in (2 * (bit % 3), 2 * (bit % 3) + 1):
            t = OPPOSITE[s + 1]
            tap = slice(t * 256, (t + 1) * 256)
            td_ref[:, tap] = td_ref[:, tap] + dot(place_ref[bit, s % 2], fr3[bit]).astype(BF16)
    pump(runs)
    back = upstream
    for t in range(7):
        tap = slice(t * 256, (t + 1) * 256)
        back = back + dot_nt(td_ref[:, tap], w2_ref[tap, :])
    grad_coarse = back.astype(BF16)

    grad_down = dot(patcht_ref[...], grad_coarse)
    fill(
        chains[2].total, jnp.concatenate([grad_down[:, 0:128], grad_down[:, 128:256]], axis=0)
    )
    pump(runs)
    runs.append(chains[2].steps())
    pump(runs[2:])
    for c in range(8):
        cols = slice(c * 128, (c + 1) * 128)
        patch_grad = dot_nt(grad_coarse, dw_ref[cols, :])
        delta1_ref[c * rows : (c + 1) * rows, :] = (patch_grad * slope_ref[:, cols]).astype(BF16)
    pump(runs)
    fill(chains[3].total, dot(t1t_ref[...], delta1_ref[...]))
    runs.append(chains[3].steps())
    pump(runs[3:])
    while runs:
        pump(runs)


CUT = 2048


def fill(ref, value):
    ref[0 : value.shape[0], :] = value
    if ref.shape[0] > value.shape[0]:
        ref[value.shape[0] :, :] = jnp.zeros((ref.shape[0] - value.shape[0], 128), F32)


def pump(runs):
    for run in list(runs):
        if next(run, "end") == "end":
            runs.remove(run)


def finish(*refs):
    incoming, (enc_out, one_out, down_out, two_out), held = refs[:5], refs[5:9], refs[9:14]
    one_ref, down_ref, two_ref, load_sems, sems = refs[14:]
    loads = [
        pltpu.make_async_copy(src, dst, load_sems.at[k])
        for k, (src, dst) in enumerate(zip(incoming, held))
    ]
    for k in (0, 1, 2, 3, 4):
        loads[k].start()
    a_ref, b_ref, c_ref, d_ref, enc_ref = held
    copies = []

    def send(src, dst):
        copies.append(pltpu.make_async_copy(src, dst, sems.at[len(copies)]))
        copies[-1].start()

    loads[0].wait()
    loads[1].wait()
    for t in range(7):
        at = slice(t * 256, (t + 1) * 256)
        two_ref[at, 0:128] = a_ref[at, :].astype(F32)
        low = 1792 + t * 256
        right = a_ref[low : low + 256, :] if low < CUT else b_ref[low - CUT : low - CUT + 256, :]
        two_ref[at, 128:256] = right.astype(F32)
        send(two_ref.at[at], two_out.at[at])
    loads[2].wait()
    for part in range(4):
        at = slice(part * 256, (part + 1) * 256)
        down_ref[at, 0:128] = c_ref[at, :].astype(F32)
        down_ref[at, 128:256] = c_ref[1024 + part * 256 : 1280 + part * 256, :].astype(F32)
        send(down_ref.at[at], down_out.at[at])
    loads[3].wait()
    one_ref[...] = d_ref[0:896, :].astype(F32)
    send(one_ref, one_out)
    loads[4].wait()
    send(enc_ref, enc_out)
    for one in copies:
        one.wait()


def padded(rows, devices):
    return -(-rows // (16 * devices)) * 16 * devices


def on_device(n_scene, n_kd, features, send_faces, face_source, cotangent, conv_one, down, conv_two):
    bricks = features.shape[1]
    n_bits = send_faces.shape[2]
    rows = bricks * 64
    devices = n_scene * n_kd
    scene_bits = n_scene.bit_length() - 1
    sizes = [padded(n, devices) for n in (CUT, 2 * 7 * 256 - CUT, 2 * 1024, 7 * 128)]
    n_sems = 2 * scene_bits + 2 * (n_kd - 1)
    vmem = pl.BlockSpec(memory_space=pltpu.VMEM)
    smem = pl.BlockSpec(memory_space=pltpu.SMEM)
    hbm = pl.BlockSpec(memory_space=pltpu.HBM)

    def reduction(size):
        return [
            pltpu.VMEM((size, 128), F32),
            pltpu.VMEM((size, 128), BF16),
            pltpu.VMEM((size, 128), BF16),
            pltpu.SemaphoreType.DMA((n_sems,)),
            pltpu.SemaphoreType.DMA((n_sems,)),
        ]

    encoded, *sums = pl.pallas_call(
        functools.partial(kernel, n_scene, n_kd, n_bits),
        out_shape=[jax.ShapeDtypeStruct((rows, 256), BF16)]
        + [jax.ShapeDtypeStruct((size, 128), BF16) for size in sizes],
        in_specs=[hbm, smem, smem, hbm, hbm, hbm, hbm],
        out_specs=[vmem] * 5,
        scratch_shapes=[
            pltpu.VMEM((bricks * 512, 128), BF16),
            pltpu.VMEM((rows, 256), BF16),
            pltpu.VMEM((7 * 128, 128), BF16),
            pltpu.VMEM((1024, 256), BF16),
            pltpu.VMEM((7 * 256, 256), BF16),
            pltpu.SemaphoreType.DMA((5,)),
            pltpu.VMEM((rows, 1024), BF16),
            pltpu.VMEM((8, rows, 7 * 128), BF16),
            pltpu.VMEM((7 * 128, 8 * rows), BF16),
            pltpu.VMEM((rows, 1024), F32),
            pltpu.VMEM((rows, 1024), BF16),
            pltpu.VMEM((1024, rows), BF16),
            pltpu.VMEM((8 * rows, 128), BF16),
            pltpu.VMEM((6, rows, rows), BF16),
            pltpu.VMEM((n_bits, 2, rows, 16), BF16),
            pltpu.VMEM((n_bits * 16, rows), BF16),
            pltpu.VMEM((rows, 7 * 256), BF16),
            pltpu.VMEM((rows, 7 * 256), BF16),
            pltpu.VMEM((n_bits, 16, 512), BF16),
            pltpu.VMEM((n_bits, 16, 512), BF16),
            pltpu.VMEM((n_bits, 16, 256), BF16),
            pltpu.VMEM((n_bits, 16, 256), BF16),
            pltpu.VMEM((n_bits, 16, 256), BF16),
            pltpu.VMEM((n_bits, 16, 256), BF16),
            pltpu.SemaphoreType.DMA((3 * n_bits,)),
            pltpu.SemaphoreType.DMA((3 * n_bits,)),
        ]
        + [entry for size in sizes for entry in reduction(size)],
        compiler_params=pltpu.CompilerParams(
            collective_id=0, has_side_effects=True, vmem_limit_bytes=61 * 2**20
        ),
    )(
        features.reshape(bricks * 512, 128),
        send_faces.reshape(1, n_bits),
        face_source,
        cotangent.reshape(rows, 256),
        conv_one.reshape(7 * 128, 128),
        down,
        conv_two.reshape(7 * 256, 256),
    )
    encoded, grad_one, grad_down, grad_two = pl.pallas_call(
        finish,
        out_shape=(
            jax.ShapeDtypeStruct((rows, 256), BF16),
            jax.ShapeDtypeStruct((7 * 128, 128), F32),
            jax.ShapeDtypeStruct((1024, 256), F32),
            jax.ShapeDtypeStruct((7 * 256, 256), F32),
        ),
        in_specs=[hbm] * 5,
        out_specs=(hbm,) * 4,
        scratch_shapes=[pltpu.VMEM((size, 128), BF16) for size in sizes]
        + [
            pltpu.VMEM((rows, 256), BF16),
            pltpu.VMEM((7 * 128, 128), F32),
            pltpu.VMEM((1024, 256), F32),
            pltpu.VMEM((7 * 256, 256), F32),
            pltpu.SemaphoreType.DMA((5,)),
            pltpu.SemaphoreType.DMA((13,)),
        ],
        compiler_params=pltpu.CompilerParams(vmem_limit_bytes=61 * 2**20),
    )(*sums, encoded)
    return (
        encoded.reshape(1, bricks, 64, 256),
        grad_one.reshape(7, 128, 128),
        grad_down,
        grad_two.reshape(7, 256, 256),
    )


def solution(mesh):
    placed = (
        P("scene", "kd", None, None),
        P("scene", "kd", None, None),
        P("scene", "kd", None),
        P("scene", "kd", None, None),
        P(),
        P(),
        P(),
    )
    return jax.shard_map(
        functools.partial(on_device, mesh.shape["scene"], mesh.shape["kd"]),
        mesh=mesh,
        in_specs=placed,
        out_specs=(P("scene", "kd", None, None), P(), P(), P()),
        check_vma=False,
    )
```

```python
import functools

import jax
import jax.numpy as jnp
from jax import lax
from jax.experimental import pallas as pl
from jax.experimental.pallas import tpu as pltpu
from jax.sharding import PartitionSpec as P

MESH = pl.DeviceIdType.MESH
F32 = jnp.float32
BF16 = jnp.bfloat16
STRIDE = (16, 4, 1)
CLASS = (4, 2, 1)
OPPOSITE = (0, 2, 1, 4, 3, 6, 5)


def dot(a, b):
    return jnp.dot(a, b, preferred_element_type=F32)


def dot_tn(a, b):
    return lax.dot_general(a, b, (((0,), (0,)), ((), ())), preferred_element_type=F32)


def dot_nt(a, b):
    return lax.dot_general(a, b, (((1,), (1,)), ((), ())), preferred_element_type=F32)


def one_hot(mask):
    return jnp.where(mask, 1.0, 0.0).astype(BF16)


def sigmoid(v):
    return 0.5 * jnp.tanh(0.5 * v) + 0.5


def coordinate(row, axis):
    return (row // STRIDE[axis]) % 4


def face_rows(row, axis):
    first, second = [a for a in range(3) if a != axis]
    return coordinate(row, first) * 4 + coordinate(row, second)


def lanes(ref, classes):
    return jnp.concatenate([ref[:, c * 128 : (c + 1) * 128] for c in classes], axis=1)


class Reduction:
    def __init__(self, total, staged, landed, out, sems, groups, n_scene, n_kd):
        self.total, self.staged, self.landed, self.out = total, staged, landed, out
        self.send, self.recv = sems
        self.groups, self.n_kd = groups, n_kd
        self.piece = total.shape[0] // (n_scene * n_kd)
        self.scene = lax.axis_index("scene")
        self.kd = lax.axis_index("kd")
        self.sem = 0
        self.base = 0
        self.count = n_scene * n_kd
        self.offset = 0
        self.levels = []
        self.copies = []

    def rows(self, start, count):
        return pl.ds(pl.multiple_of(start * self.piece, 16), count * self.piece)

    def copy(self, src, dst, device):
        made = pltpu.make_async_remote_copy(
            src_ref=src,
            dst_ref=dst,
            send_sem=self.send.at[self.sem],
            recv_sem=self.recv.at[self.sem],
            device_id=device,
            device_id_type=MESH,
        )
        self.sem += 1
        made.start()
        return made

    def steps(self):
        for group in self.groups:
            share = self.count >> len(group)
            digit = self.digit(group, 0)
            keep = self.offset + digit * share
            made = []
            for j in range(1, 2 ** len(group)):
                away = self.offset + self.digit(group, j) * share
                slot = pl.ds(self.base * self.piece, share * self.piece)
                self.staged[slot, :] = self.total[self.rows(away, share), :].astype(BF16)
                other = {"scene": flipped(self.scene, group, j)}
                made.append((self.copy(self.staged.at[slot], self.landed.at[slot], other), slot))
                self.base += share
            yield
            kept = self.rows(keep, share)
            value = self.total[kept, :]
            for one, slot in made:
                one.wait()
                value = value + self.landed[slot, :].astype(F32)
            self.total[kept, :] = value
            self.count = share
            self.offset = keep
            self.levels.append((group, keep, share))
        made = []
        for j in range(1, self.n_kd):
            peer = self.peer(j)
            slot = pl.ds(self.base * self.piece, self.piece)
            self.staged[slot, :] = self.total[self.rows(self.offset + peer, 1), :].astype(BF16)
            made.append((self.copy(self.staged.at[slot], self.landed.at[slot], {"kd": peer}), slot))
            self.base += 1
        yield
        own = self.rows(self.offset + self.kd, 1)
        value = self.total[own, :]
        for one, slot in made:
            one.wait()
            value = value + self.landed[slot, :].astype(F32)
        self.out[own, :] = value.astype(BF16)
        made = [
            self.copy(self.out.at[own], self.out.at[own], {"kd": self.peer(j)})
            for j in range(1, self.n_kd)
        ]
        yield
        for one in made:
            one.wait()
        for group, keep, share in reversed(self.levels):
            kept = self.rows(keep, share)
            made = [
                self.copy(
                    self.out.at[kept], self.out.at[kept], {"scene": flipped(self.scene, group, j)}
                )
                for j in range(1, 2 ** len(group))
            ]
            yield
            for one in made:
                one.wait()

    def digit(self, group, j):
        result = 0
        for place, bit in enumerate(group):
            own = (self.scene // 2**bit) % 2
            result = result + 2**place * (1 - own if j >> place & 1 else own)
        return result

    def peer(self, j):
        return flipped(self.kd, range(self.n_kd.bit_length() - 1), j)


def flipped(index, bits, j):
    result = index
    for place, bit in enumerate(bits):
        if j >> place & 1:
            result = result + 2**bit - 2 * 2**bit * ((index // 2**bit) % 2)
    return result


def groups_of(scene_bits, chain):
    chips = list(range(1, scene_bits))
    if chain >= 2:
        rest = [chips[i : i + 2] for i in range(0, len(chips), 2)]
    else:
        rest = [[bit] for bit in (chips if chain == 0 else chips[::-1])]
    return [[0]] + rest


def kernel(n_scene, n_kd, n_bits, *refs):
    refs = list(refs)

    def take(count):
        taken = refs[:count]
        del refs[:count]
        return taken

    x_hbm, send_ref, source_ref, cot_hbm, w1_hbm, dw_hbm, w2_hbm = take(7)
    enc_ref, *outs = take(5)
    x_ref, cot_ref, w1_ref, dw_ref, w2_ref, in_sem = take(6)
    xp_ref, t1_ref, t1t_ref, slope_ref, patch_ref, patcht_ref, delta1_ref = take(7)
    shift_ref, place_ref, pick_ref, t2_ref, td_ref, xt_ref, arrived_ref = take(7)
    fs1, fr1, fs2, fr2, fs3, fr3, face_send, face_recv = take(8)
    bricks = source_ref.shape[1]
    rows = bricks * 64
    local = bricks * 6
    scene_bits = n_scene.bit_length() - 1
    kd = lax.axis_index("kd")
    scene = lax.axis_index("scene")
    greeted = set()
    chains = []
    for k in range(4):
        total, staged, landed, send, recv = take(5)
        groups = groups_of(scene_bits, k)
        for group in groups:
            greeted |= {
                sum(2**bit for place, bit in enumerate(group) if j >> place & 1)
                for j in range(1, 2 ** len(group))
            }
        chains.append(
            Reduction(total, staged, landed, outs[k], (send, recv), groups, n_scene, n_kd)
        )
    loads = []
    for k, (src, dst) in enumerate(
        ((x_hbm, x_ref), (w1_hbm, w1_ref), (dw_hbm, dw_ref), (w2_hbm, w2_ref), (cot_hbm, cot_ref))
    ):
        loads.append(pltpu.make_async_copy(src, dst, in_sem.at[k]))
        loads[-1].start()
    load_x, load_w1, load_dw, load_w2, load_cot = loads

    barrier = pltpu.get_barrier_semaphore()
    for j in range(1, n_kd):
        peer = chains[0].peer(j)
        pl.semaphore_signal(barrier, inc=1, device_id={"kd": peer}, device_id_type=MESH)
    for j in sorted(greeted):
        other = flipped(scene, range(scene_bits), j)
        pl.semaphore_signal(barrier, inc=1, device_id={"scene": other}, device_id_type=MESH)

    to = lax.broadcasted_iota(jnp.int32, (128, 128), 0)
    frm = lax.broadcasted_iota(jnp.int32, (128, 128), 1)
    wanted = (
        (to // 64) * 64
        + (2 * ((to // 4) % 4) + (to // 32) % 2) * 8
        + 2 * (to % 4)
        + (to // 16) % 2
    )
    arrange = one_hot(frm == wanted)

    face = lax.broadcasted_iota(jnp.int32, (16, rows), 0)
    voxel = lax.broadcasted_iota(jnp.int32, (16, rows), 1)
    for bit in range(n_bits):
        axis = bit % 3
        mine = (kd // 2**bit) % 2
        first, second = [a for a in range(3) if a != axis]
        at = (
            (send_ref[0, bit] // 6) * 64
            + 3 * STRIDE[axis] * (1 - mine)
            + (face // 4) * STRIDE[first]
            + (face % 4) * STRIDE[second]
        )
        pick_ref[bit * 16 : (bit + 1) * 16, :] = one_hot(voxel == at)

    load_x.wait()
    for block in range(rows // 16):
        moved = dot(arrange, x_ref[block * 128 : (block + 1) * 128, :]).astype(BF16)
        for c in range(8):
            xp_ref[block * 16 : (block + 1) * 16, c * 128 : (c + 1) * 128] = moved[
                c * 16 : (c + 1) * 16
            ]

    def exchange(stage, send_buf, recv_buf, pieces):
        copies = []
        for bit in range(n_bits):
            send_buf[bit] = pieces[bit].astype(BF16)
            made = pltpu.make_async_remote_copy(
                src_ref=send_buf.at[bit],
                dst_ref=recv_buf.at[bit],
                send_sem=face_send.at[stage * n_bits + bit],
                recv_sem=face_recv.at[stage * n_bits + bit],
                device_id={"kd": chains[0].peer(2**bit)},
                device_id_type=MESH,
            )
            made.start()
            copies.append(made)
        return copies

    far = {}
    for axis in range(3):
        far[2 * axis] = [c for c in range(8) if c & CLASS[axis]]
        far[2 * axis + 1] = [c for c in range(8) if not c & CLASS[axis]]
    picked = dot(pick_ref[...], xp_ref[...])
    pieces = []
    for bit in range(n_bits):
        axis = bit % 3
        mine = (kd // 2**bit) % 2
        part = picked[bit * 16 : (bit + 1) * 16]
        pieces.append(
            jnp.where(mine == 0, lanes(part, far[2 * axis]), lanes(part, far[2 * axis + 1]))
        )
    pl.semaphore_wait(barrier, n_kd - 1 + len(greeted))
    copies = exchange(0, fs1, fr1, pieces)

    row = lax.broadcasted_iota(jnp.int32, (64, rows), 0)
    col = lax.broadcasted_iota(jnp.int32, (64, rows), 1)
    gap = col - row
    for s in range(6):
        axis, step = s // 2, STRIDE[s // 2]
        sign = 1 if s % 2 else -1
        border = coordinate(row, axis) == (3 if s % 2 else 0)
        for b in range(bricks):
            source = source_ref[0, b, s]
            base = jnp.where(source < local, (source // 6) * 64, -4096)
            wish = jnp.where(border, base - sign * 3 * step, b * 64 + sign * step)
            shift_ref[s, b * 64 : (b + 1) * 64, :] = one_hot(gap == wish)
    row16 = lax.broadcasted_iota(jnp.int32, (64, 16), 0)
    col16 = lax.broadcasted_iota(jnp.int32, (64, 16), 1)
    arriving = []
    for bit in range(n_bits):
        axis = bit % 3
        mine = (kd // 2**bit) % 2
        side = 2 * axis + 1 - mine
        arriving.append((axis, mine, side))
        border = coordinate(row16, axis) == 3 * (1 - mine)
        gap = col16 - face_rows(row16, axis)
        for b in range(bricks):
            here = jnp.where(source_ref[0, b, side] == local + bit, 0, -4096)
            place_ref[bit, b * 64 : (b + 1) * 64, :] = one_hot(gap == jnp.where(border, here, -4096))

    def tap_at(tap, width):
        return pl.ds(pl.multiple_of(tap * width, width), width)

    for c in range(8):
        t1_ref[c, :, 0:128] = xp_ref[:, c * 128 : (c + 1) * 128]
    for s in range(6):
        tap = slice((s + 1) * 128, (s + 2) * 128)
        moved = dot(shift_ref[s], lanes(xp_ref, far[s])).astype(BF16)
        for k, c in enumerate(far[s]):
            near = c ^ CLASS[s // 2]
            t1_ref[c, :, tap] = xp_ref[:, near * 128 : (near + 1) * 128]
            t1_ref[near, :, tap] = moved[:, k * 128 : (k + 1) * 128]
    for made in copies:
        made.wait()
    for bit, (axis, mine, side) in enumerate(arriving):
        tap = tap_at(side + 1, 128)
        moved = dot(place_ref[bit], fr1[bit]).astype(BF16)
        arrived_ref[bit] = moved
        for k, c in enumerate(far[2 * axis + 1]):
            near = c + CLASS[axis] * (1 - mine)
            t1_ref[near, :, tap] = t1_ref[near, :, tap] + moved[:, k * 128 : (k + 1) * 128]

    load_w1.wait()
    pre_one = dot(t1_ref[...].reshape(8 * rows, 7 * 128), w1_ref[...])
    for c in range(8):
        cols = slice(c * 128, (c + 1) * 128)
        pre = pre_one[c * rows : (c + 1) * rows]
        g = sigmoid(pre)
        slope_ref[:, cols] = g * (1.0 + pre * (1.0 - g))
        patch_ref[:, cols] = (xp_ref[:, cols].astype(F32) + pre * g).astype(BF16)

    load_dw.wait()
    coarse = dot(patch_ref[...], dw_ref[...]).astype(BF16)
    picked = dot(pick_ref[...], coarse)
    copies = exchange(1, fs2, fr2, [picked[i * 16 : (i + 1) * 16] for i in range(n_bits)])
    t2_ref[:, 0:256] = coarse
    for s in range(6):
        t2_ref[:, (s + 1) * 256 : (s + 2) * 256] = dot(shift_ref[s], coarse).astype(BF16)
    for c in range(8):
        xt_ref[c * 128 : (c + 1) * 128, :] = xp_ref[:, c * 128 : (c + 1) * 128].T
        patcht_ref[c * 128 : (c + 1) * 128, :] = patch_ref[:, c * 128 : (c + 1) * 128].T
        t1t_ref[0:128, c * rows : (c + 1) * rows] = xt_ref[c * 128 : (c + 1) * 128, :]
    for s in range(6):
        tap = slice((s + 1) * 128, (s + 2) * 128)
        operand = jnp.concatenate([xt_ref[c * 128 : (c + 1) * 128, :] for c in far[s]], axis=0)
        moved = dot(operand, shift_ref[s ^ 1]).astype(BF16)
        for k, c in enumerate(far[s]):
            near = c ^ CLASS[s // 2]
            t1t_ref[tap, c * rows : (c + 1) * rows] = xt_ref[near * 128 : (near + 1) * 128, :]
            t1t_ref[tap, near * rows : (near + 1) * rows] = moved[k * 128 : (k + 1) * 128]
    for bit, (axis, mine, side) in enumerate(arriving):
        tap = tap_at(side + 1, 128)
        for k, c in enumerate(far[2 * axis + 1]):
            at = tap_at(c + CLASS[axis] * (1 - mine), rows)
            moved = arrived_ref[bit, :, k * 128 : (k + 1) * 128].T
            t1t_ref[tap, at] = t1t_ref[tap, at] + moved
    for made in copies:
        made.wait()
    for bit, (axis, mine, side) in enumerate(arriving):
        tap = tap_at(side + 1, 256)
        t2_ref[:, tap] = t2_ref[:, tap] + dot(place_ref[bit], fr2[bit]).astype(BF16)
    load_w2.wait()
    load_cot.wait()
    pre = dot(t2_ref[...], w2_ref[...])
    g = sigmoid(pre)
    enc_ref[...] = (coarse.astype(F32) + pre * g).astype(BF16)
    upstream = cot_ref[...].astype(F32)
    delta = (upstream * (g * (1.0 + pre * (1.0 - g)))).astype(BF16)
    picked = dot(pick_ref[...], delta)
    copies = exchange(2, fs3, fr3, [picked[i * 16 : (i + 1) * 16] for i in range(n_bits)])

    grad_two = dot_tn(t2_ref[...], delta)
    flat = jnp.concatenate([grad_two[:, 0:128], grad_two[:, 128:256]], axis=0)
    fill(chains[0].total, flat[0:CUT])
    fill(chains[1].total, flat[CUT:])
    runs = [chains[0].steps(), chains[1].steps()]
    pump(runs)

    td_ref[:, 0:256] = delta
    for s in range(6):
        t = OPPOSITE[s + 1]
        td_ref[:, t * 256 : (t + 1) * 256] = dot(shift_ref[s], delta).astype(BF16)
    for made in copies:
        made.wait()
    for bit, (axis, mine, side) in enumerate(arriving):
        tap = tap_at(2 * axis + mine + 1, 256)
        td_ref[:, tap] = td_ref[:, tap] + dot(place_ref[bit], fr3[bit]).astype(BF16)
    pump(runs)
    back = upstream
    for t in range(7):
        tap = slice(t * 256, (t + 1) * 256)
        back = back + dot_nt(td_ref[:, tap], w2_ref[tap, :])
    grad_coarse = back.astype(BF16)

    grad_down = dot(patcht_ref[...], grad_coarse)
    fill(
        chains[2].total, jnp.concatenate([grad_down[:, 0:128], grad_down[:, 128:256]], axis=0)
    )
    runs.append(chains[2].steps())
    pump(runs[2:])
    for c in range(8):
        cols = slice(c * 128, (c + 1) * 128)
        patch_grad = dot_nt(grad_coarse, dw_ref[cols, :])
        delta1_ref[c * rows : (c + 1) * rows, :] = (patch_grad * slope_ref[:, cols]).astype(BF16)
    pump(runs)
    fill(chains[3].total, dot(t1t_ref[...], delta1_ref[...]))
    runs.append(chains[3].steps())
    pump(runs[3:])
    while runs:
        pump(runs)


CUT = 2048


def fill(ref, value):
    ref[0 : value.shape[0], :] = value
    if ref.shape[0] > value.shape[0]:
        ref[value.shape[0] :, :] = jnp.zeros((ref.shape[0] - value.shape[0], 128), F32)


def pump(runs):
    for run in list(runs):
        if next(run, "end") == "end":
            runs.remove(run)


def finish(*refs):
    incoming, (enc_out, one_out, down_out, two_out), held = refs[:5], refs[5:9], refs[9:14]
    one_ref, down_ref, two_ref, load_sems, sems = refs[14:]
    loads = [
        pltpu.make_async_copy(src, dst, load_sems.at[k])
        for k, (src, dst) in enumerate(zip(incoming, held))
    ]
    for k in (0, 1, 2, 3, 4):
        loads[k].start()
    a_ref, b_ref, c_ref, d_ref, enc_ref = held
    copies = []

    def send(src, dst):
        copies.append(pltpu.make_async_copy(src, dst, sems.at[len(copies)]))
        copies[-1].start()

    loads[0].wait()
    loads[1].wait()
    for t in range(7):
        at = slice(t * 256, (t + 1) * 256)
        two_ref[at, 0:128] = a_ref[at, :].astype(F32)
        low = 1792 + t * 256
        right = a_ref[low : low + 256, :] if low < CUT else b_ref[low - CUT : low - CUT + 256, :]
        two_ref[at, 128:256] = right.astype(F32)
        send(two_ref.at[at], two_out.at[at])
    loads[2].wait()
    for part in range(4):
        at = slice(part * 256, (part + 1) * 256)
        down_ref[at, 0:128] = c_ref[at, :].astype(F32)
        down_ref[at, 128:256] = c_ref[1024 + part * 256 : 1280 + part * 256, :].astype(F32)
        send(down_ref.at[at], down_out.at[at])
    loads[3].wait()
    one_ref[...] = d_ref[0:896, :].astype(F32)
    send(one_ref, one_out)
    loads[4].wait()
    send(enc_ref, enc_out)
    for one in copies:
        one.wait()


def padded(rows, devices):
    return -(-rows // (16 * devices)) * 16 * devices


def on_device(n_scene, n_kd, features, send_faces, face_source, cotangent, conv_one, down, conv_two):
    bricks = features.shape[1]
    n_bits = send_faces.shape[2]
    rows = bricks * 64
    devices = n_scene * n_kd
    scene_bits = n_scene.bit_length() - 1
    sizes = [padded(n, devices) for n in (CUT, 2 * 7 * 256 - CUT, 2 * 1024, 7 * 128)]
    exchanges = [
        n_kd - 1 + sum(2 ** len(group) - 1 for group in groups_of(scene_bits, k)) for k in range(4)
    ]
    vmem = pl.BlockSpec(memory_space=pltpu.VMEM)
    smem = pl.BlockSpec(memory_space=pltpu.SMEM)
    hbm = pl.BlockSpec(memory_space=pltpu.HBM)

    def reduction(size, count):
        return [
            pltpu.VMEM((size, 128), F32),
            pltpu.VMEM((size, 128), BF16),
            pltpu.VMEM((size, 128), BF16),
            pltpu.SemaphoreType.DMA((2 * count,)),
            pltpu.SemaphoreType.DMA((2 * count,)),
        ]

    encoded, *sums = pl.pallas_call(
        functools.partial(kernel, n_scene, n_kd, n_bits),
        out_shape=[jax.ShapeDtypeStruct((rows, 256), BF16)]
        + [jax.ShapeDtypeStruct((size, 128), BF16) for size in sizes],
        in_specs=[hbm, smem, smem, hbm, hbm, hbm, hbm],
        out_specs=[vmem] * 5,
        scratch_shapes=[
            pltpu.VMEM((bricks * 512, 128), BF16),
            pltpu.VMEM((rows, 256), BF16),
            pltpu.VMEM((7 * 128, 128), BF16),
            pltpu.VMEM((1024, 256), BF16),
            pltpu.VMEM((7 * 256, 256), BF16),
            pltpu.SemaphoreType.DMA((5,)),
            pltpu.VMEM((rows, 1024), BF16),
            pltpu.VMEM((8, rows, 7 * 128), BF16),
            pltpu.VMEM((7 * 128, 8 * rows), BF16),
            pltpu.VMEM((rows, 1024), F32),
            pltpu.VMEM((rows, 1024), BF16),
            pltpu.VMEM((1024, rows), BF16),
            pltpu.VMEM((8 * rows, 128), BF16),
            pltpu.VMEM((6, rows, rows), BF16),
            pltpu.VMEM((n_bits, rows, 16), BF16),
            pltpu.VMEM((n_bits * 16, rows), BF16),
            pltpu.VMEM((rows, 7 * 256), BF16),
            pltpu.VMEM((rows, 7 * 256), BF16),
            pltpu.VMEM((1024, rows), BF16),
            pltpu.VMEM((n_bits, rows, 512), BF16),
            pltpu.VMEM((n_bits, 16, 512), BF16),
            pltpu.VMEM((n_bits, 16, 512), BF16),
            pltpu.VMEM((n_bits, 16, 256), BF16),
            pltpu.VMEM((n_bits, 16, 256), BF16),
            pltpu.VMEM((n_bits, 16, 256), BF16),
            pltpu.VMEM((n_bits, 16, 256), BF16),
            pltpu.SemaphoreType.DMA((3 * n_bits,)),
            pltpu.SemaphoreType.DMA((3 * n_bits,)),
        ]
        + [entry for pair in zip(sizes, exchanges) for entry in reduction(*pair)],
        compiler_params=pltpu.CompilerParams(
            collective_id=0, has_side_effects=True, vmem_limit_bytes=61 * 2**20
        ),
    )(
        features.reshape(bricks * 512, 128),
        send_faces.reshape(1, n_bits),
        face_source,
        cotangent.reshape(rows, 256),
        conv_one.reshape(7 * 128, 128),
        down,
        conv_two.reshape(7 * 256, 256),
    )
    encoded, grad_one, grad_down, grad_two = pl.pallas_call(
        finish,
        out_shape=(
            jax.ShapeDtypeStruct((rows, 256), BF16),
            jax.ShapeDtypeStruct((7 * 128, 128), F32),
            jax.ShapeDtypeStruct((1024, 256), F32),
            jax.ShapeDtypeStruct((7 * 256, 256), F32),
        ),
        in_specs=[hbm] * 5,
        out_specs=(hbm,) * 4,
        scratch_shapes=[pltpu.VMEM((size, 128), BF16) for size in sizes]
        + [
            pltpu.VMEM((rows, 256), BF16),
            pltpu.VMEM((7 * 128, 128), F32),
            pltpu.VMEM((1024, 256), F32),
            pltpu.VMEM((7 * 256, 256), F32),
            pltpu.SemaphoreType.DMA((5,)),
            pltpu.SemaphoreType.DMA((13,)),
        ],
        compiler_params=pltpu.CompilerParams(vmem_limit_bytes=61 * 2**20),
    )(*sums, encoded)
    return (
        encoded.reshape(1, bricks, 64, 256),
        grad_one.reshape(7, 128, 128),
        grad_down,
        grad_two.reshape(7, 256, 256),
    )


def solution(mesh):
    placed = (
        P("scene", "kd", None, None),
        P("scene", "kd", None, None),
        P("scene", "kd", None),
        P("scene", "kd", None, None),
        P(),
        P(),
        P(),
    )
    return jax.shard_map(
        functools.partial(on_device, mesh.shape["scene"], mesh.shape["kd"]),
        mesh=mesh,
        in_specs=placed,
        out_specs=(P("scene", "kd", None, None), P(), P(), P()),
        check_vma=False,
    )
```

```python
import functools

import jax
import jax.numpy as jnp
from jax import lax
from jax.experimental import pallas as pl
from jax.experimental.pallas import tpu as pltpu
from jax.sharding import PartitionSpec as P

MESH = pl.DeviceIdType.MESH
F32 = jnp.float32
BF16 = jnp.bfloat16
STRIDE = (16, 4, 1)
CLASS = (4, 2, 1)
OPPOSITE = (0, 2, 1, 4, 3, 6, 5)


def dot(a, b):
    return jnp.dot(a, b, preferred_element_type=F32)


def dot_tn(a, b):
    return lax.dot_general(a, b, (((0,), (0,)), ((), ())), preferred_element_type=F32)


def dot_nt(a, b):
    return lax.dot_general(a, b, (((1,), (1,)), ((), ())), preferred_element_type=F32)


def one_hot(mask):
    return jnp.where(mask, 1.0, 0.0).astype(BF16)


def sigmoid(v):
    return 0.5 * jnp.tanh(0.5 * v) + 0.5


def coordinate(row, axis):
    return (row // STRIDE[axis]) % 4


def face_rows(row, axis):
    first, second = [a for a in range(3) if a != axis]
    return coordinate(row, first) * 4 + coordinate(row, second)


def lanes(ref, classes):
    return jnp.concatenate([ref[:, c * 128 : (c + 1) * 128] for c in classes], axis=1)


class Reduction:
    def __init__(self, total, staged, landed, out, store, sems, groups, n_scene, n_kd):
        self.store = store
        self.total, self.staged, self.landed, self.out = total, staged, landed, out
        self.send, self.recv = sems
        self.groups, self.n_kd = groups, n_kd
        self.piece = total.shape[0] // (n_scene * n_kd)
        self.scene = lax.axis_index("scene")
        self.kd = lax.axis_index("kd")
        self.sem = 0
        self.base = 0
        self.count = n_scene * n_kd
        self.offset = 0
        self.levels = []
        self.copies = []

    def rows(self, start, count):
        return pl.ds(pl.multiple_of(start * self.piece, 16), count * self.piece)

    def copy(self, src, dst, device):
        made = pltpu.make_async_remote_copy(
            src_ref=src,
            dst_ref=dst,
            send_sem=self.send.at[self.sem],
            recv_sem=self.recv.at[self.sem],
            device_id=device,
            device_id_type=MESH,
        )
        self.sem += 1
        made.start()
        return made

    def steps(self):
        for group in self.groups:
            share = self.count >> len(group)
            digit = self.digit(group, 0)
            keep = self.offset + digit * share
            made = []
            for j in range(1, 2 ** len(group)):
                away = self.offset + self.digit(group, j) * share
                slot = pl.ds(self.base * self.piece, share * self.piece)
                self.staged[slot, :] = self.total[self.rows(away, share), :].astype(BF16)
                other = {"scene": flipped(self.scene, group, j)}
                made.append((self.copy(self.staged.at[slot], self.landed.at[slot], other), slot))
                self.base += share
            yield
            kept = self.rows(keep, share)
            value = self.total[kept, :]
            for one, slot in made:
                one.wait()
                value = value + self.landed[slot, :].astype(F32)
            self.total[kept, :] = value
            self.count = share
            self.offset = keep
            self.levels.append((group, keep, share))
        made = []
        for j in range(1, self.n_kd):
            peer = self.peer(j)
            slot = pl.ds(self.base * self.piece, self.piece)
            self.staged[slot, :] = self.total[self.rows(self.offset + peer, 1), :].astype(BF16)
            made.append((self.copy(self.staged.at[slot], self.landed.at[slot], {"kd": peer}), slot))
            self.base += 1
        yield
        own = self.rows(self.offset + self.kd, 1)
        value = self.total[own, :]
        for one, slot in made:
            one.wait()
            value = value + self.landed[slot, :].astype(F32)
        self.out[own, :] = value.astype(BF16)
        made = [
            self.copy(self.out.at[own], self.out.at[own], {"kd": self.peer(j)})
            for j in range(1, self.n_kd)
        ]
        yield
        for one in made:
            one.wait()
        for group, keep, share in reversed(self.levels):
            kept = self.rows(keep, share)
            made = [
                self.copy(
                    self.out.at[kept], self.out.at[kept], {"scene": flipped(self.scene, group, j)}
                )
                for j in range(1, 2 ** len(group))
            ]
            yield
            for one in made:
                one.wait()
        self.store.start()

    def digit(self, group, j):
        result = 0
        for place, bit in enumerate(group):
            own = (self.scene // 2**bit) % 2
            result = result + 2**place * (1 - own if j >> place & 1 else own)
        return result

    def peer(self, j):
        return flipped(self.kd, range(self.n_kd.bit_length() - 1), j)


def flipped(index, bits, j):
    result = index
    for place, bit in enumerate(bits):
        if j >> place & 1:
            result = result + 2**bit - 2 * 2**bit * ((index // 2**bit) % 2)
    return result


def groups_of(scene_bits):
    return [[0]] + [list(range(i, min(i + 2, scene_bits))) for i in range(1, scene_bits, 2)]


def kernel(n_scene, n_kd, n_bits, *refs):
    refs = list(refs)

    def take(count):
        taken = refs[:count]
        del refs[:count]
        return taken

    x_hbm, send_ref, source_ref, cot_hbm, w1_hbm, dw_hbm, w2_hbm = take(7)
    enc_hbm, *results = take(5)
    x_ref, cot_ref, w1_ref, dw_ref, w2_ref, in_sem = take(6)
    enc_ref, out_sem, *outs = take(6)
    xp_ref, t1_ref, t1t_ref, slope_ref, patch_ref, patcht_ref, delta1_ref = take(7)
    shift_ref, place_ref, pick_ref, t2_ref, td_ref, xt_ref, arrived_ref = take(7)
    fs1, fr1, fs2, fr2, fs3, fr3, face_send, face_recv = take(8)
    bricks = source_ref.shape[1]
    rows = bricks * 64
    local = bricks * 6
    scene_bits = n_scene.bit_length() - 1
    kd = lax.axis_index("kd")
    scene = lax.axis_index("scene")
    greeted = set()
    chains = []
    for k in range(4):
        total, staged, landed, send, recv = take(5)
        groups = groups_of(scene_bits)
        for group in groups:
            greeted |= {
                sum(2**bit for place, bit in enumerate(group) if j >> place & 1)
                for j in range(1, 2 ** len(group))
            }
        chains.append(
            Reduction(
                total,
                staged,
                landed,
                outs[k],
                pltpu.make_async_copy(outs[k], results[k], out_sem.at[k]),
                (send, recv),
                groups,
                n_scene,
                n_kd,
            )
        )
    loads = []
    for k, (src, dst) in enumerate(
        ((x_hbm, x_ref), (w1_hbm, w1_ref), (dw_hbm, dw_ref), (w2_hbm, w2_ref), (cot_hbm, cot_ref))
    ):
        loads.append(pltpu.make_async_copy(src, dst, in_sem.at[k]))
        loads[-1].start()
    load_x, load_w1, load_dw, load_w2, load_cot = loads

    barrier = pltpu.get_barrier_semaphore()
    for j in range(1, n_kd):
        peer = chains[0].peer(j)
        pl.semaphore_signal(barrier, inc=1, device_id={"kd": peer}, device_id_type=MESH)
    for j in sorted(greeted):
        other = flipped(scene, range(scene_bits), j)
        pl.semaphore_signal(barrier, inc=1, device_id={"scene": other}, device_id_type=MESH)

    to = lax.broadcasted_iota(jnp.int32, (128, 128), 0)
    frm = lax.broadcasted_iota(jnp.int32, (128, 128), 1)
    wanted = (
        (to // 64) * 64
        + (2 * ((to // 4) % 4) + (to // 32) % 2) * 8
        + 2 * (to % 4)
        + (to // 16) % 2
    )
    arrange = one_hot(frm == wanted)

    face = lax.broadcasted_iota(jnp.int32, (16, rows), 0)
    voxel = lax.broadcasted_iota(jnp.int32, (16, rows), 1)
    for bit in range(n_bits):
        axis = bit % 3
        mine = (kd // 2**bit) % 2
        first, second = [a for a in range(3) if a != axis]
        at = (
            (send_ref[0, bit] // 6) * 64
            + 3 * STRIDE[axis] * (1 - mine)
            + (face // 4) * STRIDE[first]
            + (face % 4) * STRIDE[second]
        )
        pick_ref[bit * 16 : (bit + 1) * 16, :] = one_hot(voxel == at)

    load_x.wait()
    for block in range(rows // 16):
        moved = dot(arrange, x_ref[block * 128 : (block + 1) * 128, :]).astype(BF16)
        for c in range(8):
            xp_ref[block * 16 : (block + 1) * 16, c * 128 : (c + 1) * 128] = moved[
                c * 16 : (c + 1) * 16
            ]

    def exchange(stage, send_buf, recv_buf, pieces):
        copies = []
        for bit in range(n_bits):
            send_buf[bit] = pieces[bit].astype(BF16)
            made = pltpu.make_async_remote_copy(
                src_ref=send_buf.at[bit],
                dst_ref=recv_buf.at[bit],
                send_sem=face_send.at[stage * n_bits + bit],
                recv_sem=face_recv.at[stage * n_bits + bit],
                device_id={"kd": chains[0].peer(2**bit)},
                device_id_type=MESH,
            )
            made.start()
            copies.append(made)
        return copies

    far = {}
    for axis in range(3):
        far[2 * axis] = [c for c in range(8) if c & CLASS[axis]]
        far[2 * axis + 1] = [c for c in range(8) if not c & CLASS[axis]]
    picked = dot(pick_ref[...], xp_ref[...])
    pieces = []
    for bit in range(n_bits):
        axis = bit % 3
        mine = (kd // 2**bit) % 2
        part = picked[bit * 16 : (bit + 1) * 16]
        pieces.append(
            jnp.where(mine == 0, lanes(part, far[2 * axis]), lanes(part, far[2 * axis + 1]))
        )
    pl.semaphore_wait(barrier, n_kd - 1 + len(greeted))
    copies = exchange(0, fs1, fr1, pieces)

    row = lax.broadcasted_iota(jnp.int32, (64, rows), 0)
    col = lax.broadcasted_iota(jnp.int32, (64, rows), 1)
    gap = col - row
    for s in range(6):
        axis, step = s // 2, STRIDE[s // 2]
        sign = 1 if s % 2 else -1
        border = coordinate(row, axis) == (3 if s % 2 else 0)
        for b in range(bricks):
            source = source_ref[0, b, s]
            base = jnp.where(source < local, (source // 6) * 64, -4096)
            wish = jnp.where(border, base - sign * 3 * step, b * 64 + sign * step)
            shift_ref[s, b * 64 : (b + 1) * 64, :] = one_hot(gap == wish)
    row16 = lax.broadcasted_iota(jnp.int32, (64, 16), 0)
    col16 = lax.broadcasted_iota(jnp.int32, (64, 16), 1)
    arriving = []
    for bit in range(n_bits):
        axis = bit % 3
        mine = (kd // 2**bit) % 2
        side = 2 * axis + 1 - mine
        arriving.append((axis, mine, side))
        border = coordinate(row16, axis) == 3 * (1 - mine)
        gap = col16 - face_rows(row16, axis)
        for b in range(bricks):
            here = jnp.where(source_ref[0, b, side] == local + bit, 0, -4096)
            place_ref[bit, b * 64 : (b + 1) * 64, :] = one_hot(gap == jnp.where(border, here, -4096))

    def tap_at(tap, width):
        return pl.ds(pl.multiple_of(tap * width, width), width)

    for c in range(8):
        t1_ref[c, :, 0:128] = xp_ref[:, c * 128 : (c + 1) * 128]
    for s in range(6):
        tap = slice((s + 1) * 128, (s + 2) * 128)
        moved = dot(shift_ref[s], lanes(xp_ref, far[s])).astype(BF16)
        for k, c in enumerate(far[s]):
            near = c ^ CLASS[s // 2]
            t1_ref[c, :, tap] = xp_ref[:, near * 128 : (near + 1) * 128]
            t1_ref[near, :, tap] = moved[:, k * 128 : (k + 1) * 128]
    for made in copies:
        made.wait()
    for bit, (axis, mine, side) in enumerate(arriving):
        tap = tap_at(side + 1, 128)
        moved = dot(place_ref[bit], fr1[bit]).astype(BF16)
        arrived_ref[bit] = moved
        for k, c in enumerate(far[2 * axis + 1]):
            near = c + CLASS[axis] * (1 - mine)
            t1_ref[near, :, tap] = t1_ref[near, :, tap] + moved[:, k * 128 : (k + 1) * 128]

    load_w1.wait()
    pre_one = dot(t1_ref[...].reshape(8 * rows, 7 * 128), w1_ref[...])
    for c in range(8):
        cols = slice(c * 128, (c + 1) * 128)
        pre = pre_one[c * rows : (c + 1) * rows]
        g = sigmoid(pre)
        slope_ref[:, cols] = g * (1.0 + pre * (1.0 - g))
        patch_ref[:, cols] = (xp_ref[:, cols].astype(F32) + pre * g).astype(BF16)

    load_dw.wait()
    coarse = dot(patch_ref[...], dw_ref[...]).astype(BF16)
    picked = dot(pick_ref[...], coarse)
    copies = exchange(1, fs2, fr2, [picked[i * 16 : (i + 1) * 16] for i in range(n_bits)])
    t2_ref[:, 0:256] = coarse
    for s in range(6):
        t2_ref[:, (s + 1) * 256 : (s + 2) * 256] = dot(shift_ref[s], coarse).astype(BF16)
    for c in range(8):
        xt_ref[c * 128 : (c + 1) * 128, :] = xp_ref[:, c * 128 : (c + 1) * 128].T
        patcht_ref[c * 128 : (c + 1) * 128, :] = patch_ref[:, c * 128 : (c + 1) * 128].T
        t1t_ref[0:128, c * rows : (c + 1) * rows] = xt_ref[c * 128 : (c + 1) * 128, :]
    for s in range(6):
        tap = slice((s + 1) * 128, (s + 2) * 128)
        operand = jnp.concatenate([xt_ref[c * 128 : (c + 1) * 128, :] for c in far[s]], axis=0)
        moved = dot(operand, shift_ref[s ^ 1]).astype(BF16)
        for k, c in enumerate(far[s]):
            near = c ^ CLASS[s // 2]
            t1t_ref[tap, c * rows : (c + 1) * rows] = xt_ref[near * 128 : (near + 1) * 128, :]
            t1t_ref[tap, near * rows : (near + 1) * rows] = moved[k * 128 : (k + 1) * 128]
    for bit, (axis, mine, side) in enumerate(arriving):
        tap = tap_at(side + 1, 128)
        for k, c in enumerate(far[2 * axis + 1]):
            at = tap_at(c + CLASS[axis] * (1 - mine), rows)
            moved = arrived_ref[bit, :, k * 128 : (k + 1) * 128].T
            t1t_ref[tap, at] = t1t_ref[tap, at] + moved
    for made in copies:
        made.wait()
    for bit, (axis, mine, side) in enumerate(arriving):
        tap = tap_at(side + 1, 256)
        t2_ref[:, tap] = t2_ref[:, tap] + dot(place_ref[bit], fr2[bit]).astype(BF16)
    load_w2.wait()
    load_cot.wait()
    pre = dot(t2_ref[...], w2_ref[...])
    g = sigmoid(pre)
    enc_ref[...] = (coarse.astype(F32) + pre * g).astype(BF16)
    store_enc = pltpu.make_async_copy(enc_ref, enc_hbm, out_sem.at[4])
    store_enc.start()
    upstream = cot_ref[...].astype(F32)
    delta = (upstream * (g * (1.0 + pre * (1.0 - g)))).astype(BF16)
    picked = dot(pick_ref[...], delta)
    copies = exchange(2, fs3, fr3, [picked[i * 16 : (i + 1) * 16] for i in range(n_bits)])

    grad_two = dot_tn(t2_ref[...], delta)
    flat = jnp.concatenate([grad_two[:, 0:128], grad_two[:, 128:256]], axis=0)
    fill(chains[0].total, flat[0:CUT])
    fill(chains[1].total, flat[CUT:])
    runs = [chains[0].steps(), chains[1].steps()]
    pump(runs)

    td_ref[:, 0:256] = delta
    for s in range(6):
        t = OPPOSITE[s + 1]
        td_ref[:, t * 256 : (t + 1) * 256] = dot(shift_ref[s], delta).astype(BF16)
    for made in copies:
        made.wait()
    for bit, (axis, mine, side) in enumerate(arriving):
        tap = tap_at(2 * axis + mine + 1, 256)
        td_ref[:, tap] = td_ref[:, tap] + dot(place_ref[bit], fr3[bit]).astype(BF16)
    pump(runs)
    back = upstream
    for t in range(7):
        tap = slice(t * 256, (t + 1) * 256)
        back = back + dot_nt(td_ref[:, tap], w2_ref[tap, :])
    grad_coarse = back.astype(BF16)

    grad_down = dot(patcht_ref[...], grad_coarse)
    fill(
        chains[2].total, jnp.concatenate([grad_down[:, 0:128], grad_down[:, 128:256]], axis=0)
    )
    runs.append(chains[2].steps())
    pump(runs[2:])
    for c in range(8):
        cols = slice(c * 128, (c + 1) * 128)
        patch_grad = dot_nt(grad_coarse, dw_ref[cols, :])
        delta1_ref[c * rows : (c + 1) * rows, :] = (patch_grad * slope_ref[:, cols]).astype(BF16)
    pump(runs[2:])
    fill(chains[3].total, dot(t1t_ref[...], delta1_ref[...]))
    runs.append(chains[3].steps())
    pump(runs[3:])
    while runs:
        pump(runs)
    store_enc.wait()
    for chain in chains:
        chain.store.wait()


CUT = 2048


def fill(ref, value):
    ref[0 : value.shape[0], :] = value
    if ref.shape[0] > value.shape[0]:
        ref[value.shape[0] :, :] = jnp.zeros((ref.shape[0] - value.shape[0], 128), F32)


def pump(runs):
    for run in list(runs):
        if next(run, "end") == "end":
            runs.remove(run)


def finish(*refs):
    incoming, (enc_out, one_out, down_out, two_out), held = refs[:5], refs[5:9], refs[9:14]
    one_ref, down_ref, two_ref, load_sems, sems = refs[14:]
    loads = [
        pltpu.make_async_copy(src, dst, load_sems.at[k])
        for k, (src, dst) in enumerate(zip(incoming, held))
    ]
    for k in (0, 1, 2, 3, 4):
        loads[k].start()
    a_ref, b_ref, c_ref, d_ref, enc_ref = held
    copies = []

    def send(src, dst):
        copies.append(pltpu.make_async_copy(src, dst, sems.at[len(copies)]))
        copies[-1].start()

    loads[0].wait()
    loads[1].wait()
    for t in range(7):
        at = slice(t * 256, (t + 1) * 256)
        two_ref[at, 0:128] = a_ref[at, :].astype(F32)
        low = 1792 + t * 256
        right = a_ref[low : low + 256, :] if low < CUT else b_ref[low - CUT : low - CUT + 256, :]
        two_ref[at, 128:256] = right.astype(F32)
        send(two_ref.at[at], two_out.at[at])
    loads[2].wait()
    for part in range(4):
        at = slice(part * 256, (part + 1) * 256)
        down_ref[at, 0:128] = c_ref[at, :].astype(F32)
        down_ref[at, 128:256] = c_ref[1024 + part * 256 : 1280 + part * 256, :].astype(F32)
        send(down_ref.at[at], down_out.at[at])
    loads[3].wait()
    one_ref[...] = d_ref[0:896, :].astype(F32)
    send(one_ref, one_out)
    loads[4].wait()
    send(enc_ref, enc_out)
    for one in copies:
        one.wait()


def padded(rows, devices):
    return -(-rows // (16 * devices)) * 16 * devices


def on_device(n_scene, n_kd, features, send_faces, face_source, cotangent, conv_one, down, conv_two):
    bricks = features.shape[1]
    n_bits = send_faces.shape[2]
    rows = bricks * 64
    devices = n_scene * n_kd
    scene_bits = n_scene.bit_length() - 1
    sizes = [padded(n, devices) for n in (CUT, 2 * 7 * 256 - CUT, 2 * 1024, 7 * 128)]
    exchanges = [
        n_kd - 1 + sum(2 ** len(group) - 1 for group in groups_of(scene_bits)) for _ in sizes
    ]
    smem = pl.BlockSpec(memory_space=pltpu.SMEM)
    hbm = pl.BlockSpec(memory_space=pltpu.HBM)

    def reduction(size, count):
        return [
            pltpu.VMEM((size, 128), F32),
            pltpu.VMEM((size, 128), BF16),
            pltpu.VMEM((size, 128), BF16),
            pltpu.SemaphoreType.DMA((2 * count,)),
            pltpu.SemaphoreType.DMA((2 * count,)),
        ]

    encoded, *sums = pl.pallas_call(
        functools.partial(kernel, n_scene, n_kd, n_bits),
        out_shape=[jax.ShapeDtypeStruct((rows, 256), BF16)]
        + [jax.ShapeDtypeStruct((size, 128), BF16) for size in sizes],
        in_specs=[hbm, smem, smem, hbm, hbm, hbm, hbm],
        out_specs=[hbm] * 5,
        scratch_shapes=[
            pltpu.VMEM((bricks * 512, 128), BF16),
            pltpu.VMEM((rows, 256), BF16),
            pltpu.VMEM((7 * 128, 128), BF16),
            pltpu.VMEM((1024, 256), BF16),
            pltpu.VMEM((7 * 256, 256), BF16),
            pltpu.SemaphoreType.DMA((5,)),
            pltpu.VMEM((rows, 256), BF16),
            pltpu.SemaphoreType.DMA((5,)),
        ]
        + [pltpu.VMEM((size, 128), BF16) for size in sizes]
        + [
            pltpu.VMEM((rows, 1024), BF16),
            pltpu.VMEM((8, rows, 7 * 128), BF16),
            pltpu.VMEM((7 * 128, 8 * rows), BF16),
            pltpu.VMEM((rows, 1024), F32),
            pltpu.VMEM((rows, 1024), BF16),
            pltpu.VMEM((1024, rows), BF16),
            pltpu.VMEM((8 * rows, 128), BF16),
            pltpu.VMEM((6, rows, rows), BF16),
            pltpu.VMEM((n_bits, rows, 16), BF16),
            pltpu.VMEM((n_bits * 16, rows), BF16),
            pltpu.VMEM((rows, 7 * 256), BF16),
            pltpu.VMEM((rows, 7 * 256), BF16),
            pltpu.VMEM((1024, rows), BF16),
            pltpu.VMEM((n_bits, rows, 512), BF16),
            pltpu.VMEM((n_bits, 16, 512), BF16),
            pltpu.VMEM((n_bits, 16, 512), BF16),
            pltpu.VMEM((n_bits, 16, 256), BF16),
            pltpu.VMEM((n_bits, 16, 256), BF16),
            pltpu.VMEM((n_bits, 16, 256), BF16),
            pltpu.VMEM((n_bits, 16, 256), BF16),
            pltpu.SemaphoreType.DMA((3 * n_bits,)),
            pltpu.SemaphoreType.DMA((3 * n_bits,)),
        ]
        + [entry for pair in zip(sizes, exchanges) for entry in reduction(*pair)],
        compiler_params=pltpu.CompilerParams(
            collective_id=0, has_side_effects=True, vmem_limit_bytes=61 * 2**20
        ),
    )(
        features.reshape(bricks * 512, 128),
        send_faces.reshape(1, n_bits),
        face_source,
        cotangent.reshape(rows, 256),
        conv_one.reshape(7 * 128, 128),
        down,
        conv_two.reshape(7 * 256, 256),
    )
    encoded, grad_one, grad_down, grad_two = pl.pallas_call(
        finish,
        out_shape=(
            jax.ShapeDtypeStruct((rows, 256), BF16),
            jax.ShapeDtypeStruct((7 * 128, 128), F32),
            jax.ShapeDtypeStruct((1024, 256), F32),
            jax.ShapeDtypeStruct((7 * 256, 256), F32),
        ),
        in_specs=[hbm] * 5,
        out_specs=(hbm,) * 4,
        scratch_shapes=[pltpu.VMEM((size, 128), BF16) for size in sizes]
        + [
            pltpu.VMEM((rows, 256), BF16),
            pltpu.VMEM((7 * 128, 128), F32),
            pltpu.VMEM((1024, 256), F32),
            pltpu.VMEM((7 * 256, 256), F32),
            pltpu.SemaphoreType.DMA((5,)),
            pltpu.SemaphoreType.DMA((13,)),
        ],
        compiler_params=pltpu.CompilerParams(vmem_limit_bytes=61 * 2**20),
    )(*sums, encoded)
    return (
        encoded.reshape(1, bricks, 64, 256),
        grad_one.reshape(7, 128, 128),
        grad_down,
        grad_two.reshape(7, 256, 256),
    )


def solution(mesh):
    placed = (
        P("scene", "kd", None, None),
        P("scene", "kd", None, None),
        P("scene", "kd", None),
        P("scene", "kd", None, None),
        P(),
        P(),
        P(),
    )
    return jax.shard_map(
        functools.partial(on_device, mesh.shape["scene"], mesh.shape["kd"]),
        mesh=mesh,
        in_specs=placed,
        out_specs=(P("scene", "kd", None, None), P(), P(), P()),
        check_vma=False,
    )
```

```python
import functools

import jax
import jax.numpy as jnp
from jax import lax
from jax.experimental import pallas as pl
from jax.experimental.pallas import tpu as pltpu
from jax.sharding import PartitionSpec as P

MESH = pl.DeviceIdType.MESH
F32 = jnp.float32
BF16 = jnp.bfloat16
STRIDE = (16, 4, 1)
CLASS = (4, 2, 1)
OPPOSITE = (0, 2, 1, 4, 3, 6, 5)


def dot(a, b):
    return jnp.dot(a, b, preferred_element_type=F32)


def dot_nt(a, b):
    return lax.dot_general(a, b, (((1,), (1,)), ((), ())), preferred_element_type=F32)


def turned(identity, a):
    return dot_nt(identity, a).astype(BF16)


def one_hot(mask):
    return jnp.where(mask, 1.0, 0.0).astype(BF16)


def sigmoid(v):
    return 0.5 * jnp.tanh(0.5 * v) + 0.5


def coordinate(row, axis):
    return (row // STRIDE[axis]) % 4


def face_rows(row, axis):
    first, second = [a for a in range(3) if a != axis]
    return coordinate(row, first) * 4 + coordinate(row, second)


def lanes(ref, classes):
    return jnp.concatenate([ref[:, c * 128 : (c + 1) * 128] for c in classes], axis=1)


class Reduction:
    def __init__(self, total, staged, landed, out, store, sems, groups, n_scene, n_kd):
        self.store = store
        self.total, self.staged, self.landed, self.out = total, staged, landed, out
        self.send, self.recv = sems
        self.groups, self.n_kd = groups, n_kd
        self.piece = total.shape[0] // (n_scene * n_kd)
        self.scene = lax.axis_index("scene")
        self.kd = lax.axis_index("kd")
        self.sem = 0
        self.base = 0
        self.count = n_scene * n_kd
        self.offset = 0
        self.levels = []
        self.copies = []

    def rows(self, start, count):
        return pl.ds(pl.multiple_of(start * self.piece, 16), count * self.piece)

    def copy(self, src, dst, device):
        made = pltpu.make_async_remote_copy(
            src_ref=src,
            dst_ref=dst,
            send_sem=self.send.at[self.sem],
            recv_sem=self.recv.at[self.sem],
            device_id=device,
            device_id_type=MESH,
        )
        self.sem += 1
        made.start()
        return made

    def steps(self):
        for group in self.groups:
            share = self.count >> len(group)
            digit = self.digit(group, 0)
            keep = self.offset + digit * share
            made = []
            for j in range(1, 2 ** len(group)):
                away = self.offset + self.digit(group, j) * share
                slot = pl.ds(self.base * self.piece, share * self.piece)
                self.staged[slot, :] = self.total[self.rows(away, share), :].astype(BF16)
                other = {"scene": flipped(self.scene, group, j)}
                made.append((self.copy(self.staged.at[slot], self.landed.at[slot], other), slot))
                self.base += share
            yield
            kept = self.rows(keep, share)
            value = self.total[kept, :]
            for one, slot in made:
                one.wait()
                value = value + self.landed[slot, :].astype(F32)
            self.total[kept, :] = value
            self.count = share
            self.offset = keep
            self.levels.append((group, keep, share))
        made = []
        for j in range(1, self.n_kd):
            peer = self.peer(j)
            slot = pl.ds(self.base * self.piece, self.piece)
            self.staged[slot, :] = self.total[self.rows(self.offset + peer, 1), :].astype(BF16)
            made.append((self.copy(self.staged.at[slot], self.landed.at[slot], {"kd": peer}), slot))
            self.base += 1
        yield
        own = self.rows(self.offset + self.kd, 1)
        value = self.total[own, :]
        for one, slot in made:
            one.wait()
            value = value + self.landed[slot, :].astype(F32)
        self.out[own, :] = value.astype(BF16)
        made = [
            self.copy(self.out.at[own], self.out.at[own], {"kd": self.peer(j)})
            for j in range(1, self.n_kd)
        ]
        yield
        for one in made:
            one.wait()
        for group, keep, share in reversed(self.levels):
            kept = self.rows(keep, share)
            made = [
                self.copy(
                    self.out.at[kept], self.out.at[kept], {"scene": flipped(self.scene, group, j)}
                )
                for j in range(1, 2 ** len(group))
            ]
            yield
            for one in made:
                one.wait()
        self.store.start()

    def digit(self, group, j):
        result = 0
        for place, bit in enumerate(group):
            own = (self.scene // 2**bit) % 2
            result = result + 2**place * (1 - own if j >> place & 1 else own)
        return result

    def peer(self, j):
        return flipped(self.kd, range(self.n_kd.bit_length() - 1), j)


def flipped(index, bits, j):
    result = index
    for place, bit in enumerate(bits):
        if j >> place & 1:
            result = result + 2**bit - 2 * 2**bit * ((index // 2**bit) % 2)
    return result


def groups_of(scene_bits):
    return [[0]] + [list(range(i, min(i + 2, scene_bits))) for i in range(1, scene_bits, 2)]


def kernel(n_scene, n_kd, n_bits, *refs):
    refs = list(refs)

    def take(count):
        taken = refs[:count]
        del refs[:count]
        return taken

    x_hbm, send_ref, source_ref, cot_hbm, w1_hbm, dw_hbm, w2_hbm = take(7)
    enc_hbm, *results = take(5)
    x_ref, cot_ref, w1_ref, dw_ref, w2_ref, in_sem = take(6)
    enc_ref, out_sem, *outs = take(6)
    xp_ref, t1_ref, t1t_ref, slope_ref, patch_ref, patcht_ref, delta1_ref = take(7)
    shift_ref, place_ref, pick_ref, t2_ref, td_ref, xt_ref, arrived_ref, t2t_ref = take(8)
    fs1, fr1, fs2, fr2, fs3, fr3, face_send, face_recv = take(8)
    bricks = source_ref.shape[1]
    rows = bricks * 64
    local = bricks * 6
    scene_bits = n_scene.bit_length() - 1
    kd = lax.axis_index("kd")
    scene = lax.axis_index("scene")
    greeted = set()
    chains = []
    for k in range(4):
        total, staged, landed, send, recv = take(5)
        groups = groups_of(scene_bits)
        for group in groups:
            greeted |= {
                sum(2**bit for place, bit in enumerate(group) if j >> place & 1)
                for j in range(1, 2 ** len(group))
            }
        chains.append(
            Reduction(
                total,
                staged,
                landed,
                outs[k],
                pltpu.make_async_copy(outs[k], results[k], out_sem.at[k]),
                (send, recv),
                groups,
                n_scene,
                n_kd,
            )
        )
    loads = []
    for k, (src, dst) in enumerate(
        ((x_hbm, x_ref), (w1_hbm, w1_ref), (dw_hbm, dw_ref), (w2_hbm, w2_ref), (cot_hbm, cot_ref))
    ):
        loads.append(pltpu.make_async_copy(src, dst, in_sem.at[k]))
        loads[-1].start()
    load_x, load_w1, load_dw, load_w2, load_cot = loads

    barrier = pltpu.get_barrier_semaphore()
    for j in range(1, n_kd):
        peer = chains[0].peer(j)
        pl.semaphore_signal(barrier, inc=1, device_id={"kd": peer}, device_id_type=MESH)
    for j in sorted(greeted):
        other = flipped(scene, range(scene_bits), j)
        pl.semaphore_signal(barrier, inc=1, device_id={"scene": other}, device_id_type=MESH)

    to = lax.broadcasted_iota(jnp.int32, (128, 128), 0)
    frm = lax.broadcasted_iota(jnp.int32, (128, 128), 1)
    wanted = (
        (to // 64) * 64
        + (2 * ((to // 4) % 4) + (to // 32) % 2) * 8
        + 2 * (to % 4)
        + (to // 16) % 2
    )
    arrange = one_hot(frm == wanted)
    identity = one_hot(frm == to)

    face = lax.broadcasted_iota(jnp.int32, (16, rows), 0)
    voxel = lax.broadcasted_iota(jnp.int32, (16, rows), 1)
    for bit in range(n_bits):
        axis = bit % 3
        mine = (kd // 2**bit) % 2
        first, second = [a for a in range(3) if a != axis]
        at = (
            (send_ref[0, bit] // 6) * 64
            + 3 * STRIDE[axis] * (1 - mine)
            + (face // 4) * STRIDE[first]
            + (face % 4) * STRIDE[second]
        )
        pick_ref[bit * 16 : (bit + 1) * 16, :] = one_hot(voxel == at)

    load_x.wait()
    for block in range(rows // 16):
        moved = dot(arrange, x_ref[block * 128 : (block + 1) * 128, :]).astype(BF16)
        for c in range(8):
            xp_ref[block * 16 : (block + 1) * 16, c * 128 : (c + 1) * 128] = moved[
                c * 16 : (c + 1) * 16
            ]

    def exchange(stage, send_buf, recv_buf, pieces):
        copies = []
        for bit in range(n_bits):
            send_buf[bit] = pieces[bit].astype(BF16)
            made = pltpu.make_async_remote_copy(
                src_ref=send_buf.at[bit],
                dst_ref=recv_buf.at[bit],
                send_sem=face_send.at[stage * n_bits + bit],
                recv_sem=face_recv.at[stage * n_bits + bit],
                device_id={"kd": chains[0].peer(2**bit)},
                device_id_type=MESH,
            )
            made.start()
            copies.append(made)
        return copies

    far = {}
    for axis in range(3):
        far[2 * axis] = [c for c in range(8) if c & CLASS[axis]]
        far[2 * axis + 1] = [c for c in range(8) if not c & CLASS[axis]]
    picked = dot(pick_ref[...], xp_ref[...])
    pieces = []
    for bit in range(n_bits):
        axis = bit % 3
        mine = (kd // 2**bit) % 2
        part = picked[bit * 16 : (bit + 1) * 16]
        pieces.append(
            jnp.where(mine == 0, lanes(part, far[2 * axis]), lanes(part, far[2 * axis + 1]))
        )
    pl.semaphore_wait(barrier, n_kd - 1 + len(greeted))
    copies = exchange(0, fs1, fr1, pieces)

    row = lax.broadcasted_iota(jnp.int32, (64, rows), 0)
    col = lax.broadcasted_iota(jnp.int32, (64, rows), 1)
    gap = col - row
    for s in range(6):
        axis, step = s // 2, STRIDE[s // 2]
        sign = 1 if s % 2 else -1
        border = coordinate(row, axis) == (3 if s % 2 else 0)
        for b in range(bricks):
            source = source_ref[0, b, s]
            base = jnp.where(source < local, (source // 6) * 64, -4096)
            wish = jnp.where(border, base - sign * 3 * step, b * 64 + sign * step)
            shift_ref[s, b * 64 : (b + 1) * 64, :] = one_hot(gap == wish)
    row16 = lax.broadcasted_iota(jnp.int32, (64, 16), 0)
    col16 = lax.broadcasted_iota(jnp.int32, (64, 16), 1)
    arriving = []
    for bit in range(n_bits):
        axis = bit % 3
        mine = (kd // 2**bit) % 2
        side = 2 * axis + 1 - mine
        arriving.append((axis, mine, side))
        border = coordinate(row16, axis) == 3 * (1 - mine)
        gap = col16 - face_rows(row16, axis)
        for b in range(bricks):
            here = jnp.where(source_ref[0, b, side] == local + bit, 0, -4096)
            place_ref[bit, b * 64 : (b + 1) * 64, :] = one_hot(gap == jnp.where(border, here, -4096))

    def tap_at(tap, width):
        return pl.ds(pl.multiple_of(tap * width, width), width)

    for c in range(8):
        t1_ref[c, :, 0:128] = xp_ref[:, c * 128 : (c + 1) * 128]
    for s in range(6):
        tap = slice((s + 1) * 128, (s + 2) * 128)
        moved = dot(shift_ref[s], lanes(xp_ref, far[s])).astype(BF16)
        for k, c in enumerate(far[s]):
            near = c ^ CLASS[s // 2]
            t1_ref[c, :, tap] = xp_ref[:, near * 128 : (near + 1) * 128]
            t1_ref[near, :, tap] = moved[:, k * 128 : (k + 1) * 128]
    for made in copies:
        made.wait()
    for bit, (axis, mine, side) in enumerate(arriving):
        tap = tap_at(side + 1, 128)
        moved = dot(place_ref[bit], fr1[bit]).astype(BF16)
        arrived_ref[bit] = moved
        for k, c in enumerate(far[2 * axis + 1]):
            near = c + CLASS[axis] * (1 - mine)
            t1_ref[near, :, tap] = t1_ref[near, :, tap] + moved[:, k * 128 : (k + 1) * 128]

    load_w1.wait()
    pre_one = dot(t1_ref[...].reshape(8 * rows, 7 * 128), w1_ref[...])
    for c in range(8):
        cols = slice(c * 128, (c + 1) * 128)
        pre = pre_one[c * rows : (c + 1) * rows]
        g = sigmoid(pre)
        slope_ref[:, cols] = g * (1.0 + pre * (1.0 - g))
        patch_ref[:, cols] = (xp_ref[:, cols].astype(F32) + pre * g).astype(BF16)

    load_dw.wait()
    coarse = dot(patch_ref[...], dw_ref[...]).astype(BF16)
    picked = dot(pick_ref[...], coarse)
    copies = exchange(1, fs2, fr2, [picked[i * 16 : (i + 1) * 16] for i in range(n_bits)])
    t2_ref[:, 0:256] = coarse
    for s in range(6):
        t2_ref[:, (s + 1) * 256 : (s + 2) * 256] = dot(shift_ref[s], coarse).astype(BF16)
    for c in range(8):
        xt_ref[c * 128 : (c + 1) * 128, :] = turned(
            identity, xp_ref[:, c * 128 : (c + 1) * 128]
        )
        patcht_ref[c * 128 : (c + 1) * 128, :] = turned(
            identity, patch_ref[:, c * 128 : (c + 1) * 128]
        )
        t1t_ref[0:128, c * rows : (c + 1) * rows] = xt_ref[c * 128 : (c + 1) * 128, :]
    for s in range(6):
        tap = slice((s + 1) * 128, (s + 2) * 128)
        operand = jnp.concatenate([xt_ref[c * 128 : (c + 1) * 128, :] for c in far[s]], axis=0)
        moved = dot(operand, shift_ref[s ^ 1]).astype(BF16)
        for k, c in enumerate(far[s]):
            near = c ^ CLASS[s // 2]
            t1t_ref[tap, c * rows : (c + 1) * rows] = xt_ref[near * 128 : (near + 1) * 128, :]
            t1t_ref[tap, near * rows : (near + 1) * rows] = moved[k * 128 : (k + 1) * 128]
    for bit, (axis, mine, side) in enumerate(arriving):
        tap = tap_at(side + 1, 128)
        for k, c in enumerate(far[2 * axis + 1]):
            at = tap_at(c + CLASS[axis] * (1 - mine), rows)
            moved = turned(identity, arrived_ref[bit, :, k * 128 : (k + 1) * 128])
            t1t_ref[tap, at] = t1t_ref[tap, at] + moved
    for made in copies:
        made.wait()
    for bit, (axis, mine, side) in enumerate(arriving):
        tap = tap_at(side + 1, 256)
        t2_ref[:, tap] = t2_ref[:, tap] + dot(place_ref[bit], fr2[bit]).astype(BF16)
    load_w2.wait()
    load_cot.wait()
    pre = dot(t2_ref[...], w2_ref[...])
    g = sigmoid(pre)
    enc_ref[...] = (coarse.astype(F32) + pre * g).astype(BF16)
    store_enc = pltpu.make_async_copy(enc_ref, enc_hbm, out_sem.at[4])
    store_enc.start()
    upstream = cot_ref[...].astype(F32)
    delta = (upstream * (g * (1.0 + pre * (1.0 - g)))).astype(BF16)
    picked = dot(pick_ref[...], delta)
    copies = exchange(2, fs3, fr3, [picked[i * 16 : (i + 1) * 16] for i in range(n_bits)])

    for k in range(14):
        at = slice(k * 128, (k + 1) * 128)
        t2t_ref[at, :] = turned(identity, t2_ref[:, at])
    grad_two = dot(t2t_ref[...], delta)
    flat = jnp.concatenate([grad_two[:, 0:128], grad_two[:, 128:256]], axis=0)
    fill(chains[0].total, flat[0:CUT])
    fill(chains[1].total, flat[CUT:])
    runs = [chains[0].steps(), chains[1].steps()]
    pump(runs)

    td_ref[:, 0:256] = delta
    for s in range(6):
        t = OPPOSITE[s + 1]
        td_ref[:, t * 256 : (t + 1) * 256] = dot(shift_ref[s], delta).astype(BF16)
    for made in copies:
        made.wait()
    for bit, (axis, mine, side) in enumerate(arriving):
        tap = tap_at(2 * axis + mine + 1, 256)
        td_ref[:, tap] = td_ref[:, tap] + dot(place_ref[bit], fr3[bit]).astype(BF16)
    pump(runs)
    back = upstream
    for t in range(7):
        tap = slice(t * 256, (t + 1) * 256)
        back = back + dot_nt(td_ref[:, tap], w2_ref[tap, :])
    grad_coarse = back.astype(BF16)

    grad_down = dot(patcht_ref[...], grad_coarse)
    fill(
        chains[2].total, jnp.concatenate([grad_down[:, 0:128], grad_down[:, 128:256]], axis=0)
    )
    runs.append(chains[2].steps())
    pump(runs[2:])
    for c in range(8):
        cols = slice(c * 128, (c + 1) * 128)
        patch_grad = dot_nt(grad_coarse, dw_ref[cols, :])
        delta1_ref[c * rows : (c + 1) * rows, :] = (patch_grad * slope_ref[:, cols]).astype(BF16)
    pump(runs[2:])
    fill(chains[3].total, dot(t1t_ref[...], delta1_ref[...]))
    runs.append(chains[3].steps())
    pump(runs[3:])
    while runs:
        pump(runs)
    store_enc.wait()
    for chain in chains:
        chain.store.wait()


CUT = 2048


def fill(ref, value):
    ref[0 : value.shape[0], :] = value
    if ref.shape[0] > value.shape[0]:
        ref[value.shape[0] :, :] = jnp.zeros((ref.shape[0] - value.shape[0], 128), F32)


def pump(runs):
    for run in list(runs):
        if next(run, "end") == "end":
            runs.remove(run)


def finish(*refs):
    incoming, (enc_out, one_out, down_out, two_out), held = refs[:5], refs[5:9], refs[9:14]
    one_ref, down_ref, two_ref, load_sems, sems = refs[14:]
    loads = [
        pltpu.make_async_copy(src, dst, load_sems.at[k])
        for k, (src, dst) in enumerate(zip(incoming, held))
    ]
    for k in (0, 1, 2, 3, 4):
        loads[k].start()
    a_ref, b_ref, c_ref, d_ref, enc_ref = held
    copies = []

    def send(src, dst):
        copies.append(pltpu.make_async_copy(src, dst, sems.at[len(copies)]))
        copies[-1].start()

    loads[0].wait()
    loads[1].wait()
    for t in range(7):
        at = slice(t * 256, (t + 1) * 256)
        two_ref[at, 0:128] = a_ref[at, :].astype(F32)
        low = 1792 + t * 256
        right = a_ref[low : low + 256, :] if low < CUT else b_ref[low - CUT : low - CUT + 256, :]
        two_ref[at, 128:256] = right.astype(F32)
        send(two_ref.at[at], two_out.at[at])
    loads[2].wait()
    for part in range(4):
        at = slice(part * 256, (part + 1) * 256)
        down_ref[at, 0:128] = c_ref[at, :].astype(F32)
        down_ref[at, 128:256] = c_ref[1024 + part * 256 : 1280 + part * 256, :].astype(F32)
        send(down_ref.at[at], down_out.at[at])
    loads[3].wait()
    one_ref[...] = d_ref[0:896, :].astype(F32)
    send(one_ref, one_out)
    loads[4].wait()
    send(enc_ref, enc_out)
    for one in copies:
        one.wait()


def padded(rows, devices):
    return -(-rows // (16 * devices)) * 16 * devices


def on_device(n_scene, n_kd, features, send_faces, face_source, cotangent, conv_one, down, conv_two):
    bricks = features.shape[1]
    n_bits = send_faces.shape[2]
    rows = bricks * 64
    devices = n_scene * n_kd
    scene_bits = n_scene.bit_length() - 1
    sizes = [padded(n, devices) for n in (CUT, 2 * 7 * 256 - CUT, 2 * 1024, 7 * 128)]
    exchanges = [
        n_kd - 1 + sum(2 ** len(group) - 1 for group in groups_of(scene_bits)) for _ in sizes
    ]
    smem = pl.BlockSpec(memory_space=pltpu.SMEM)
    hbm = pl.BlockSpec(memory_space=pltpu.HBM)

    def reduction(size, count):
        return [
            pltpu.VMEM((size, 128), F32),
            pltpu.VMEM((size, 128), BF16),
            pltpu.VMEM((size, 128), BF16),
            pltpu.SemaphoreType.DMA((2 * count,)),
            pltpu.SemaphoreType.DMA((2 * count,)),
        ]

    encoded, *sums = pl.pallas_call(
        functools.partial(kernel, n_scene, n_kd, n_bits),
        out_shape=[jax.ShapeDtypeStruct((rows, 256), BF16)]
        + [jax.ShapeDtypeStruct((size, 128), BF16) for size in sizes],
        in_specs=[hbm, smem, smem, hbm, hbm, hbm, hbm],
        out_specs=[hbm] * 5,
        scratch_shapes=[
            pltpu.VMEM((bricks * 512, 128), BF16),
            pltpu.VMEM((rows, 256), BF16),
            pltpu.VMEM((7 * 128, 128), BF16),
            pltpu.VMEM((1024, 256), BF16),
            pltpu.VMEM((7 * 256, 256), BF16),
            pltpu.SemaphoreType.DMA((5,)),
            pltpu.VMEM((rows, 256), BF16),
            pltpu.SemaphoreType.DMA((5,)),
        ]
        + [pltpu.VMEM((size, 128), BF16) for size in sizes]
        + [
            pltpu.VMEM((rows, 1024), BF16),
            pltpu.VMEM((8, rows, 7 * 128), BF16),
            pltpu.VMEM((7 * 128, 8 * rows), BF16),
            pltpu.VMEM((rows, 1024), F32),
            pltpu.VMEM((rows, 1024), BF16),
            pltpu.VMEM((1024, rows), BF16),
            pltpu.VMEM((8 * rows, 128), BF16),
            pltpu.VMEM((6, rows, rows), BF16),
            pltpu.VMEM((n_bits, rows, 16), BF16),
            pltpu.VMEM((n_bits * 16, rows), BF16),
            pltpu.VMEM((rows, 7 * 256), BF16),
            pltpu.VMEM((rows, 7 * 256), BF16),
            pltpu.VMEM((1024, rows), BF16),
            pltpu.VMEM((n_bits, rows, 512), BF16),
            pltpu.VMEM((7 * 256, rows), BF16),
            pltpu.VMEM((n_bits, 16, 512), BF16),
            pltpu.VMEM((n_bits, 16, 512), BF16),
            pltpu.VMEM((n_bits, 16, 256), BF16),
            pltpu.VMEM((n_bits, 16, 256), BF16),
            pltpu.VMEM((n_bits, 16, 256), BF16),
            pltpu.VMEM((n_bits, 16, 256), BF16),
            pltpu.SemaphoreType.DMA((3 * n_bits,)),
            pltpu.SemaphoreType.DMA((3 * n_bits,)),
        ]
        + [entry for pair in zip(sizes, exchanges) for entry in reduction(*pair)],
        compiler_params=pltpu.CompilerParams(
            collective_id=0, has_side_effects=True, vmem_limit_bytes=61 * 2**20
        ),
    )(
        features.reshape(bricks * 512, 128),
        send_faces.reshape(1, n_bits),
        face_source,
        cotangent.reshape(rows, 256),
        conv_one.reshape(7 * 128, 128),
        down,
        conv_two.reshape(7 * 256, 256),
    )
    encoded, grad_one, grad_down, grad_two = pl.pallas_call(
        finish,
        out_shape=(
            jax.ShapeDtypeStruct((rows, 256), BF16),
            jax.ShapeDtypeStruct((7 * 128, 128), F32),
            jax.ShapeDtypeStruct((1024, 256), F32),
            jax.ShapeDtypeStruct((7 * 256, 256), F32),
        ),
        in_specs=[hbm] * 5,
        out_specs=(hbm,) * 4,
        scratch_shapes=[pltpu.VMEM((size, 128), BF16) for size in sizes]
        + [
            pltpu.VMEM((rows, 256), BF16),
            pltpu.VMEM((7 * 128, 128), F32),
            pltpu.VMEM((1024, 256), F32),
            pltpu.VMEM((7 * 256, 256), F32),
            pltpu.SemaphoreType.DMA((5,)),
            pltpu.SemaphoreType.DMA((13,)),
        ],
        compiler_params=pltpu.CompilerParams(vmem_limit_bytes=61 * 2**20),
    )(*sums, encoded)
    return (
        encoded.reshape(1, bricks, 64, 256),
        grad_one.reshape(7, 128, 128),
        grad_down,
        grad_two.reshape(7, 256, 256),
    )


def solution(mesh):
    placed = (
        P("scene", "kd", None, None),
        P("scene", "kd", None, None),
        P("scene", "kd", None),
        P("scene", "kd", None, None),
        P(),
        P(),
        P(),
    )
    return jax.shard_map(
        functools.partial(on_device, mesh.shape["scene"], mesh.shape["kd"]),
        mesh=mesh,
        in_specs=placed,
        out_specs=(P("scene", "kd", None, None), P(), P(), P()),
        check_vma=False,
    )
```

```python
import functools

import jax
import jax.numpy as jnp
from jax import lax
from jax.experimental import pallas as pl
from jax.experimental.pallas import tpu as pltpu
from jax.sharding import PartitionSpec as P

MESH = pl.DeviceIdType.MESH
F32 = jnp.float32
BF16 = jnp.bfloat16
STRIDE = (16, 4, 1)
CLASS = (4, 2, 1)
OPPOSITE = (0, 2, 1, 4, 3, 6, 5)


def dot(a, b):
    return jnp.dot(a, b, preferred_element_type=F32)


def dot_nt(a, b):
    return lax.dot_general(a, b, (((1,), (1,)), ((), ())), preferred_element_type=F32)


def turned(identity, a):
    return dot_nt(identity, a).astype(BF16)


def one_hot(mask):
    return jnp.where(mask, 1.0, 0.0).astype(BF16)


def sigmoid(v):
    return 0.5 * jnp.tanh(0.5 * v) + 0.5


def coordinate(row, axis):
    return (row // STRIDE[axis]) % 4


def face_rows(row, axis):
    first, second = [a for a in range(3) if a != axis]
    return coordinate(row, first) * 4 + coordinate(row, second)


def lanes(ref, classes):
    return jnp.concatenate([ref[:, c * 128 : (c + 1) * 128] for c in classes], axis=1)


class Reduction:
    def __init__(self, total, staged, landed, out, store, sems, groups, n_scene, n_kd):
        self.store = store
        self.total, self.staged, self.landed, self.out = total, staged, landed, out
        self.send, self.recv = sems
        self.groups, self.n_kd = groups, n_kd
        self.piece = total.shape[0] // (n_scene * n_kd)
        self.scene = lax.axis_index("scene")
        self.kd = lax.axis_index("kd")
        self.sem = 0
        self.base = 0
        self.count = n_scene * n_kd
        self.offset = 0
        self.levels = []
        self.copies = []

    def rows(self, start, count):
        return pl.ds(pl.multiple_of(start * self.piece, 16), count * self.piece)

    def copy(self, src, dst, device):
        made = pltpu.make_async_remote_copy(
            src_ref=src,
            dst_ref=dst,
            send_sem=self.send.at[self.sem],
            recv_sem=self.recv.at[self.sem],
            device_id=device,
            device_id_type=MESH,
        )
        self.sem += 1
        made.start()
        return made

    def steps(self):
        for group in self.groups:
            share = self.count >> len(group)
            digit = self.digit(group, 0)
            keep = self.offset + digit * share
            made = []
            for j in range(1, 2 ** len(group)):
                away = self.offset + self.digit(group, j) * share
                slot = pl.ds(self.base * self.piece, share * self.piece)
                self.staged[slot, :] = self.total[self.rows(away, share), :].astype(BF16)
                other = {"scene": flipped(self.scene, group, j)}
                made.append((self.copy(self.staged.at[slot], self.landed.at[slot], other), slot))
                self.base += share
            yield
            kept = self.rows(keep, share)
            value = self.total[kept, :]
            for one, slot in made:
                one.wait()
                value = value + self.landed[slot, :].astype(F32)
            self.total[kept, :] = value
            self.count = share
            self.offset = keep
            self.levels.append((group, keep, share))
        made = []
        for j in range(1, self.n_kd):
            peer = self.peer(j)
            slot = pl.ds(self.base * self.piece, self.piece)
            self.staged[slot, :] = self.total[self.rows(self.offset + peer, 1), :].astype(BF16)
            made.append((self.copy(self.staged.at[slot], self.landed.at[slot], {"kd": peer}), slot))
            self.base += 1
        yield
        own = self.rows(self.offset + self.kd, 1)
        value = self.total[own, :]
        for one, slot in made:
            one.wait()
            value = value + self.landed[slot, :].astype(F32)
        self.out[own, :] = value.astype(BF16)
        made = [
            self.copy(self.out.at[own], self.out.at[own], {"kd": self.peer(j)})
            for j in range(1, self.n_kd)
        ]
        yield
        for one in made:
            one.wait()
        for group, keep, share in reversed(self.levels):
            kept = self.rows(keep, share)
            made = [
                self.copy(
                    self.out.at[kept], self.out.at[kept], {"scene": flipped(self.scene, group, j)}
                )
                for j in range(1, 2 ** len(group))
            ]
            yield
            for one in made:
                one.wait()
        self.store.start()

    def digit(self, group, j):
        result = 0
        for place, bit in enumerate(group):
            own = (self.scene // 2**bit) % 2
            result = result + 2**place * (1 - own if j >> place & 1 else own)
        return result

    def peer(self, j):
        return flipped(self.kd, range(self.n_kd.bit_length() - 1), j)


def flipped(index, bits, j):
    result = index
    for place, bit in enumerate(bits):
        if j >> place & 1:
            result = result + 2**bit - 2 * 2**bit * ((index // 2**bit) % 2)
    return result


def groups_of(scene_bits, chain):
    chips = list(range(1, scene_bits))
    if chain >= 2:
        rest = [chips[i : i + 2] for i in range(0, len(chips), 2)]
    else:
        rest = [[bit] for bit in (chips if chain == 0 else chips[::-1])]
    return [[0]] + rest


def kernel(n_scene, n_kd, n_bits, *refs):
    refs = list(refs)

    def take(count):
        taken = refs[:count]
        del refs[:count]
        return taken

    x_hbm, send_ref, source_ref, cot_hbm, w1_hbm, dw_hbm, w2_hbm = take(7)
    enc_hbm, *results = take(5)
    x_ref, cot_ref, w1_ref, dw_ref, w2_ref, in_sem = take(6)
    enc_ref, out_sem, *outs = take(6)
    xp_ref, t1_ref, t1t_ref, slope_ref, patch_ref, patcht_ref, delta1_ref = take(7)
    shift_ref, place_ref, pick_ref, t2_ref, td_ref, xt_ref, arrived_ref, t2t_ref = take(8)
    fs1, fr1, fs2, fr2, fs3, fr3, face_send, face_recv = take(8)
    bricks = source_ref.shape[1]
    rows = bricks * 64
    local = bricks * 6
    scene_bits = n_scene.bit_length() - 1
    kd = lax.axis_index("kd")
    scene = lax.axis_index("scene")
    greeted = set()
    chains = []
    for k in range(4):
        total, staged, landed, send, recv = take(5)
        groups = groups_of(scene_bits, k)
        for group in groups:
            greeted |= {
                sum(2**bit for place, bit in enumerate(group) if j >> place & 1)
                for j in range(1, 2 ** len(group))
            }
        chains.append(
            Reduction(
                total,
                staged,
                landed,
                outs[k],
                pltpu.make_async_copy(outs[k], results[k], out_sem.at[k]),
                (send, recv),
                groups,
                n_scene,
                n_kd,
            )
        )
    loads = []
    for k, (src, dst) in enumerate(
        ((x_hbm, x_ref), (w1_hbm, w1_ref), (dw_hbm, dw_ref), (w2_hbm, w2_ref), (cot_hbm, cot_ref))
    ):
        loads.append(pltpu.make_async_copy(src, dst, in_sem.at[k]))
        loads[-1].start()
    load_x, load_w1, load_dw, load_w2, load_cot = loads

    barrier = pltpu.get_barrier_semaphore()
    for j in range(1, n_kd):
        peer = chains[0].peer(j)
        pl.semaphore_signal(barrier, inc=1, device_id={"kd": peer}, device_id_type=MESH)
    for j in sorted(greeted):
        other = flipped(scene, range(scene_bits), j)
        pl.semaphore_signal(barrier, inc=1, device_id={"scene": other}, device_id_type=MESH)

    to = lax.broadcasted_iota(jnp.int32, (128, 128), 0)
    frm = lax.broadcasted_iota(jnp.int32, (128, 128), 1)
    wanted = (
        (to // 64) * 64
        + (2 * ((to // 4) % 4) + (to // 32) % 2) * 8
        + 2 * (to % 4)
        + (to // 16) % 2
    )
    arrange = one_hot(frm == wanted)
    identity = one_hot(frm == to)

    face = lax.broadcasted_iota(jnp.int32, (16, rows), 0)
    voxel = lax.broadcasted_iota(jnp.int32, (16, rows), 1)
    for bit in range(n_bits):
        axis = bit % 3
        mine = (kd // 2**bit) % 2
        first, second = [a for a in range(3) if a != axis]
        at = (
            (send_ref[0, bit] // 6) * 64
            + 3 * STRIDE[axis] * (1 - mine)
            + (face // 4) * STRIDE[first]
            + (face % 4) * STRIDE[second]
        )
        pick_ref[bit * 16 : (bit + 1) * 16, :] = one_hot(voxel == at)

    load_x.wait()
    for block in range(rows // 16):
        moved = dot(arrange, x_ref[block * 128 : (block + 1) * 128, :]).astype(BF16)
        for c in range(8):
            xp_ref[block * 16 : (block + 1) * 16, c * 128 : (c + 1) * 128] = moved[
                c * 16 : (c + 1) * 16
            ]

    def exchange(stage, send_buf, recv_buf, pieces):
        copies = []
        for bit in range(n_bits):
            send_buf[bit] = pieces[bit].astype(BF16)
            made = pltpu.make_async_remote_copy(
                src_ref=send_buf.at[bit],
                dst_ref=recv_buf.at[bit],
                send_sem=face_send.at[stage * n_bits + bit],
                recv_sem=face_recv.at[stage * n_bits + bit],
                device_id={"kd": chains[0].peer(2**bit)},
                device_id_type=MESH,
            )
            made.start()
            copies.append(made)
        return copies

    far = {}
    for axis in range(3):
        far[2 * axis] = [c for c in range(8) if c & CLASS[axis]]
        far[2 * axis + 1] = [c for c in range(8) if not c & CLASS[axis]]
    picked = dot(pick_ref[...], xp_ref[...])
    pieces = []
    for bit in range(n_bits):
        axis = bit % 3
        mine = (kd // 2**bit) % 2
        part = picked[bit * 16 : (bit + 1) * 16]
        pieces.append(
            jnp.where(mine == 0, lanes(part, far[2 * axis]), lanes(part, far[2 * axis + 1]))
        )
    pl.semaphore_wait(barrier, n_kd - 1 + len(greeted))
    copies = exchange(0, fs1, fr1, pieces)

    row = lax.broadcasted_iota(jnp.int32, (64, rows), 0)
    col = lax.broadcasted_iota(jnp.int32, (64, rows), 1)
    gap = col - row
    for s in range(6):
        axis, step = s // 2, STRIDE[s // 2]
        sign = 1 if s % 2 else -1
        border = coordinate(row, axis) == (3 if s % 2 else 0)
        for b in range(bricks):
            source = source_ref[0, b, s]
            base = jnp.where(source < local, (source // 6) * 64, -4096)
            wish = jnp.where(border, base - sign * 3 * step, b * 64 + sign * step)
            shift_ref[s, b * 64 : (b + 1) * 64, :] = one_hot(gap == wish)
    row16 = lax.broadcasted_iota(jnp.int32, (64, 16), 0)
    col16 = lax.broadcasted_iota(jnp.int32, (64, 16), 1)
    arriving = []
    for bit in range(n_bits):
        axis = bit % 3
        mine = (kd // 2**bit) % 2
        side = 2 * axis + 1 - mine
        arriving.append((axis, mine, side))
        border = coordinate(row16, axis) == 3 * (1 - mine)
        gap = col16 - face_rows(row16, axis)
        for b in range(bricks):
            here = jnp.where(source_ref[0, b, side] == local + bit, 0, -4096)
            place_ref[bit, b * 64 : (b + 1) * 64, :] = one_hot(gap == jnp.where(border, here, -4096))

    def tap_at(tap, width):
        return pl.ds(pl.multiple_of(tap * width, width), width)

    for c in range(8):
        t1_ref[c, :, 0:128] = xp_ref[:, c * 128 : (c + 1) * 128]
    for s in range(6):
        tap = slice((s + 1) * 128, (s + 2) * 128)
        moved = dot(shift_ref[s], lanes(xp_ref, far[s])).astype(BF16)
        for k, c in enumerate(far[s]):
            near = c ^ CLASS[s // 2]
            t1_ref[c, :, tap] = xp_ref[:, near * 128 : (near + 1) * 128]
            t1_ref[near, :, tap] = moved[:, k * 128 : (k + 1) * 128]
    for made in copies:
        made.wait()
    for bit, (axis, mine, side) in enumerate(arriving):
        tap = tap_at(side + 1, 128)
        moved = dot(place_ref[bit], fr1[bit]).astype(BF16)
        arrived_ref[bit] = moved
        for k, c in enumerate(far[2 * axis + 1]):
            near = c + CLASS[axis] * (1 - mine)
            t1_ref[near, :, tap] = t1_ref[near, :, tap] + moved[:, k * 128 : (k + 1) * 128]

    load_w1.wait()
    pre_one = dot(t1_ref[...].reshape(8 * rows, 7 * 128), w1_ref[...])
    for c in range(8):
        cols = slice(c * 128, (c + 1) * 128)
        pre = pre_one[c * rows : (c + 1) * rows]
        g = sigmoid(pre)
        slope_ref[:, cols] = g * (1.0 + pre * (1.0 - g))
        patch_ref[:, cols] = (xp_ref[:, cols].astype(F32) + pre * g).astype(BF16)

    load_dw.wait()
    coarse = dot(patch_ref[...], dw_ref[...]).astype(BF16)
    picked = dot(pick_ref[...], coarse)
    copies = exchange(1, fs2, fr2, [picked[i * 16 : (i + 1) * 16] for i in range(n_bits)])
    t2_ref[:, 0:256] = coarse
    for s in range(6):
        t2_ref[:, (s + 1) * 256 : (s + 2) * 256] = dot(shift_ref[s], coarse).astype(BF16)
    for c in range(8):
        xt_ref[c * 128 : (c + 1) * 128, :] = turned(
            identity, xp_ref[:, c * 128 : (c + 1) * 128]
        )
        patcht_ref[c * 128 : (c + 1) * 128, :] = turned(
            identity, patch_ref[:, c * 128 : (c + 1) * 128]
        )
        t1t_ref[0:128, c * rows : (c + 1) * rows] = xt_ref[c * 128 : (c + 1) * 128, :]
    for s in range(6):
        tap = slice((s + 1) * 128, (s + 2) * 128)
        operand = jnp.concatenate([xt_ref[c * 128 : (c + 1) * 128, :] for c in far[s]], axis=0)
        moved = dot(operand, shift_ref[s ^ 1]).astype(BF16)
        for k, c in enumerate(far[s]):
            near = c ^ CLASS[s // 2]
            t1t_ref[tap, c * rows : (c + 1) * rows] = xt_ref[near * 128 : (near + 1) * 128, :]
            t1t_ref[tap, near * rows : (near + 1) * rows] = moved[k * 128 : (k + 1) * 128]
    for bit, (axis, mine, side) in enumerate(arriving):
        tap = tap_at(side + 1, 128)
        for k, c in enumerate(far[2 * axis + 1]):
            at = tap_at(c + CLASS[axis] * (1 - mine), rows)
            moved = turned(identity, arrived_ref[bit, :, k * 128 : (k + 1) * 128])
            t1t_ref[tap, at] = t1t_ref[tap, at] + moved
    for made in copies:
        made.wait()
    for bit, (axis, mine, side) in enumerate(arriving):
        tap = tap_at(side + 1, 256)
        t2_ref[:, tap] = t2_ref[:, tap] + dot(place_ref[bit], fr2[bit]).astype(BF16)
    load_w2.wait()
    load_cot.wait()
    pre = dot(t2_ref[...], w2_ref[...])
    g = sigmoid(pre)
    enc_ref[...] = (coarse.astype(F32) + pre * g).astype(BF16)
    store_enc = pltpu.make_async_copy(enc_ref, enc_hbm, out_sem.at[4])
    store_enc.start()
    upstream = cot_ref[...].astype(F32)
    delta = (upstream * (g * (1.0 + pre * (1.0 - g)))).astype(BF16)
    picked = dot(pick_ref[...], delta)
    copies = exchange(2, fs3, fr3, [picked[i * 16 : (i + 1) * 16] for i in range(n_bits)])

    for k in range(14):
        at = slice(k * 128, (k + 1) * 128)
        t2t_ref[at, :] = turned(identity, t2_ref[:, at])
    grad_two = dot(t2t_ref[...], delta)
    flat = jnp.concatenate([grad_two[:, 0:128], grad_two[:, 128:256]], axis=0)
    fill(chains[0].total, flat[0:CUT])
    fill(chains[1].total, flat[CUT:])
    runs = [chains[0].steps(), chains[1].steps()]
    pump(runs)

    td_ref[:, 0:256] = delta
    for s in range(6):
        t = OPPOSITE[s + 1]
        td_ref[:, t * 256 : (t + 1) * 256] = dot(shift_ref[s], delta).astype(BF16)
    for made in copies:
        made.wait()
    for bit, (axis, mine, side) in enumerate(arriving):
        tap = tap_at(2 * axis + mine + 1, 256)
        td_ref[:, tap] = td_ref[:, tap] + dot(place_ref[bit], fr3[bit]).astype(BF16)
    pump(runs)
    back = upstream
    for t in range(7):
        tap = slice(t * 256, (t + 1) * 256)
        back = back + dot_nt(td_ref[:, tap], w2_ref[tap, :])
    grad_coarse = back.astype(BF16)

    grad_down = dot(patcht_ref[...], grad_coarse)
    fill(
        chains[2].total, jnp.concatenate([grad_down[:, 0:128], grad_down[:, 128:256]], axis=0)
    )
    runs.append(chains[2].steps())
    pump(runs[2:])
    for c in range(8):
        cols = slice(c * 128, (c + 1) * 128)
        patch_grad = dot_nt(grad_coarse, dw_ref[cols, :])
        delta1_ref[c * rows : (c + 1) * rows, :] = (patch_grad * slope_ref[:, cols]).astype(BF16)
    pump(runs)
    fill(chains[3].total, dot(t1t_ref[...], delta1_ref[...]))
    runs.append(chains[3].steps())
    pump(runs[3:])
    while runs:
        pump(runs)
    store_enc.wait()
    for chain in chains:
        chain.store.wait()


CUT = 2048


def fill(ref, value):
    ref[0 : value.shape[0], :] = value
    if ref.shape[0] > value.shape[0]:
        ref[value.shape[0] :, :] = jnp.zeros((ref.shape[0] - value.shape[0], 128), F32)


def pump(runs):
    for run in list(runs):
        if next(run, "end") == "end":
            runs.remove(run)


def finish(*refs):
    incoming, (enc_out, one_out, down_out, two_out), held = refs[:5], refs[5:9], refs[9:14]
    one_ref, down_ref, two_ref, load_sems, sems = refs[14:]
    loads = [
        pltpu.make_async_copy(src, dst, load_sems.at[k])
        for k, (src, dst) in enumerate(zip(incoming, held))
    ]
    for k in (0, 1, 2, 3, 4):
        loads[k].start()
    a_ref, b_ref, c_ref, d_ref, enc_ref = held
    copies = []

    def send(src, dst):
        copies.append(pltpu.make_async_copy(src, dst, sems.at[len(copies)]))
        copies[-1].start()

    loads[0].wait()
    loads[1].wait()
    for t in range(7):
        at = slice(t * 256, (t + 1) * 256)
        two_ref[at, 0:128] = a_ref[at, :].astype(F32)
        low = 1792 + t * 256
        right = a_ref[low : low + 256, :] if low < CUT else b_ref[low - CUT : low - CUT + 256, :]
        two_ref[at, 128:256] = right.astype(F32)
        send(two_ref.at[at], two_out.at[at])
    loads[2].wait()
    for part in range(4):
        at = slice(part * 256, (part + 1) * 256)
        down_ref[at, 0:128] = c_ref[at, :].astype(F32)
        down_ref[at, 128:256] = c_ref[1024 + part * 256 : 1280 + part * 256, :].astype(F32)
        send(down_ref.at[at], down_out.at[at])
    loads[3].wait()
    one_ref[...] = d_ref[0:896, :].astype(F32)
    send(one_ref, one_out)
    loads[4].wait()
    send(enc_ref, enc_out)
    for one in copies:
        one.wait()


def padded(rows, devices):
    return -(-rows // (16 * devices)) * 16 * devices


def on_device(n_scene, n_kd, features, send_faces, face_source, cotangent, conv_one, down, conv_two):
    bricks = features.shape[1]
    n_bits = send_faces.shape[2]
    rows = bricks * 64
    devices = n_scene * n_kd
    scene_bits = n_scene.bit_length() - 1
    sizes = [padded(n, devices) for n in (CUT, 2 * 7 * 256 - CUT, 2 * 1024, 7 * 128)]
    exchanges = [
        n_kd - 1 + sum(2 ** len(group) - 1 for group in groups_of(scene_bits, k)) for k in range(4)
    ]
    smem = pl.BlockSpec(memory_space=pltpu.SMEM)
    hbm = pl.BlockSpec(memory_space=pltpu.HBM)

    def reduction(size, count):
        return [
            pltpu.VMEM((size, 128), F32),
            pltpu.VMEM((size, 128), BF16),
            pltpu.VMEM((size, 128), BF16),
            pltpu.SemaphoreType.DMA((2 * count,)),
            pltpu.SemaphoreType.DMA((2 * count,)),
        ]

    encoded, *sums = pl.pallas_call(
        functools.partial(kernel, n_scene, n_kd, n_bits),
        out_shape=[jax.ShapeDtypeStruct((rows, 256), BF16)]
        + [jax.ShapeDtypeStruct((size, 128), BF16) for size in sizes],
        in_specs=[hbm, smem, smem, hbm, hbm, hbm, hbm],
        out_specs=[hbm] * 5,
        scratch_shapes=[
            pltpu.VMEM((bricks * 512, 128), BF16),
            pltpu.VMEM((rows, 256), BF16),
            pltpu.VMEM((7 * 128, 128), BF16),
            pltpu.VMEM((1024, 256), BF16),
            pltpu.VMEM((7 * 256, 256), BF16),
            pltpu.SemaphoreType.DMA((5,)),
            pltpu.VMEM((rows, 256), BF16),
            pltpu.SemaphoreType.DMA((5,)),
        ]
        + [pltpu.VMEM((size, 128), BF16) for size in sizes]
        + [
            pltpu.VMEM((rows, 1024), BF16),
            pltpu.VMEM((8, rows, 7 * 128), BF16),
            pltpu.VMEM((7 * 128, 8 * rows), BF16),
            pltpu.VMEM((rows, 1024), F32),
            pltpu.VMEM((rows, 1024), BF16),
            pltpu.VMEM((1024, rows), BF16),
            pltpu.VMEM((8 * rows, 128), BF16),
            pltpu.VMEM((6, rows, rows), BF16),
            pltpu.VMEM((n_bits, rows, 16), BF16),
            pltpu.VMEM((n_bits * 16, rows), BF16),
            pltpu.VMEM((rows, 7 * 256), BF16),
            pltpu.VMEM((rows, 7 * 256), BF16),
            pltpu.VMEM((1024, rows), BF16),
            pltpu.VMEM((n_bits, rows, 512), BF16),
            pltpu.VMEM((7 * 256, rows), BF16),
            pltpu.VMEM((n_bits, 16, 512), BF16),
            pltpu.VMEM((n_bits, 16, 512), BF16),
            pltpu.VMEM((n_bits, 16, 256), BF16),
            pltpu.VMEM((n_bits, 16, 256), BF16),
            pltpu.VMEM((n_bits, 16, 256), BF16),
            pltpu.VMEM((n_bits, 16, 256), BF16),
            pltpu.SemaphoreType.DMA((3 * n_bits,)),
            pltpu.SemaphoreType.DMA((3 * n_bits,)),
        ]
        + [entry for pair in zip(sizes, exchanges) for entry in reduction(*pair)],
        compiler_params=pltpu.CompilerParams(
            collective_id=0, has_side_effects=True, vmem_limit_bytes=61 * 2**20
        ),
    )(
        features.reshape(bricks * 512, 128),
        send_faces.reshape(1, n_bits),
        face_source,
        cotangent.reshape(rows, 256),
        conv_one.reshape(7 * 128, 128),
        down,
        conv_two.reshape(7 * 256, 256),
    )
    encoded, grad_one, grad_down, grad_two = pl.pallas_call(
        finish,
        out_shape=(
            jax.ShapeDtypeStruct((rows, 256), BF16),
            jax.ShapeDtypeStruct((7 * 128, 128), F32),
            jax.ShapeDtypeStruct((1024, 256), F32),
            jax.ShapeDtypeStruct((7 * 256, 256), F32),
        ),
        in_specs=[hbm] * 5,
        out_specs=(hbm,) * 4,
        scratch_shapes=[pltpu.VMEM((size, 128), BF16) for size in sizes]
        + [
            pltpu.VMEM((rows, 256), BF16),
            pltpu.VMEM((7 * 128, 128), F32),
            pltpu.VMEM((1024, 256), F32),
            pltpu.VMEM((7 * 256, 256), F32),
            pltpu.SemaphoreType.DMA((5,)),
            pltpu.SemaphoreType.DMA((13,)),
        ],
        compiler_params=pltpu.CompilerParams(vmem_limit_bytes=61 * 2**20),
    )(*sums, encoded)
    return (
        encoded.reshape(1, bricks, 64, 256),
        grad_one.reshape(7, 128, 128),
        grad_down,
        grad_two.reshape(7, 256, 256),
    )


def solution(mesh):
    placed = (
        P("scene", "kd", None, None),
        P("scene", "kd", None, None),
        P("scene", "kd", None),
        P("scene", "kd", None, None),
        P(),
        P(),
        P(),
    )
    return jax.shard_map(
        functools.partial(on_device, mesh.shape["scene"], mesh.shape["kd"]),
        mesh=mesh,
        in_specs=placed,
        out_specs=(P("scene", "kd", None, None), P(), P(), P()),
        check_vma=False,
    )
```
